256 devices in a mesh: dp: 64 (over y, z, core), seq: 4 (over x).
Axes of the slice: x: 4, y: 4, z: 8, core: 2. Of those that a mesh axis runs over, the one named last changes fastest.
Arguments:
- layer_in: bfloat16 [64, 1024, 4096], P('dp', 'seq'), may hold values from -6 to 6
- head_in: bfloat16 [64, 1024, 4096], P('dp', 'seq'), may hold values from -6 to 6
- ids: int32 [64, 1024], P('dp', 'seq'), may hold values from 0 to 5, never falling along the last dimension, each value on 1 to 512 neighbouring positions
- dy: bfloat16 [64, 1024, 4096], P('dp', 'seq'), may hold values from -6 to 6
- w_in: bfloat16 [4096, 320], P('dp'), may hold values from -0.09375 to 0.09375
- a_log: float32 [64], replicated, may hold values from -3 to 0.7
- dt_bias: float32 [64], replicated, may hold values from -5 to -3
- d_skip: float32 [64], replicated, may hold values from 0.5 to 1.5
Outputs:
- layer_out: bfloat16 [64, 1024, 4096], P('dp', 'seq')
- grad_x: bfloat16 [64, 1024, 4096], P('dp', 'seq')
- grad_u: bfloat16 [64, 1024, 4096], P('dp', 'seq')
- grad_w: float32 [4096, 320], P('dp')
The draws below stay inside these ranges and needn't reach their ends.
Inputs may be any that keep to these rules, and one draw needn't show every extreme that they name: `ids`: document numbers never fall along a sequence; no document is longer than 512 positions.
All inputs are finite; a program needn't handle non-finite values.
Results may differ from the reference program's by a relative error of at most 0.0049.
Values may be sent and summed in bfloat16 or wider, within the bound.
No kernel may reach another device: no remote copies, remote signals or barrier semaphores. Data moves between devices by JAX's collectives and lax.ppermute only.
A program may use at most 128 MiB of HBM per device.

```python
import math
import jax
import jax.numpy as jnp
import numpy as np
from jax import lax

D = 4096
H = 64
P_SIZE = 64
N = 128
TOK_DEV = 256
PROJ = 320
HP = 4096
LENGTH = 1024
SEQS = 64
N_SEQ = 4


def block_scale(rng, extent, split, low, high):
    level, own = 1.0, jax.random.fold_in(rng, 6)
    for position, parts in split:
        draws = jnp.exp(jax.random.uniform(jax.random.fold_in(own, position), (parts,), jnp.float32, low / len(split), high / len(split)))
        level = level * jnp.repeat(draws, extent[position] // parts).reshape([-1 if axis == position else 1 for axis in range(len(extent))])
    return level


def length_profile(number_of, total, limit, slope):
    portions = [(1 << 20) // math.isqrt(standing ** slope) + 1 for standing in range(2, number_of + 1)]
    surplus, holding = total - limit - (number_of - 1), [1] * (number_of - 1)
    while surplus > 0:
        free = [i for i in range(number_of - 1) if holding[i] < limit]
        mass, left = sum([portions[i] for i in free]), surplus
        for i in free:
            extra = min(limit - holding[i], max(1, left * portions[i] // mass), surplus)
            holding[i] = holding[i] + extra
            surplus = surplus - extra
    return np.array([limit] + holding)


def ragged_sizes(rng, count, total, most, lean):
    if count == 2:
        one = jax.random.randint(rng, (), max(1, total - most), min(most, total - 1) + 1)
        return jnp.stack([one, total - one])
    lengths = jnp.asarray(length_profile(count, total, most, lean), jnp.int32)
    twos = (count - 1) // 2
    donor, sink = lengths[1:1 + 2 * twos:2], lengths[2:2 + 2 * twos:2]
    room = jnp.minimum(donor - 1, most - sink)
    moved = jax.random.randint(jax.random.fold_in(rng, 1), (twos,), 0, 1 << 20) % (room + 1)
    lengths = lengths.at[1:1 + 2 * twos:2].set(donor - moved).at[2:2 + 2 * twos:2].set(sink + moved)
    return lengths[jax.random.permutation(jax.random.fold_in(rng, 2), count)]


def gaussian(key, shape, width, most, shards=(), kind=jnp.bfloat16):
    values = jax.random.normal(key, shape, jnp.float32) * width
    if len(shards) > 0:
        values = block_scale(key, shape, shards, -0.22, 0.18) * values
    return jnp.clip(values, min=-most, max=most).astype(kind)


def setup_inputs(seed: int = 0) -> dict:
    splits = jax.random.split(jax.random.key(seed), 9)
    return {
        "layer_in": gaussian(splits[0], (SEQS, LENGTH, D), 1.0, 6.0, ((0, 64), (1, 4))),
        "head_in": gaussian(splits[1], (SEQS, LENGTH, HP), 1.0, 6.0, ((0, 64), (1, 4))),
        "ids": jax.vmap(lambda own: jnp.searchsorted(jnp.cumsum(ragged_sizes(own, 6, LENGTH, LENGTH // 2, 1)), jnp.arange(LENGTH), side="right"))(jax.random.split(splits[2], SEQS)).reshape((SEQS, LENGTH)).astype(jnp.int32),
        "dy": gaussian(splits[3], (SEQS, LENGTH, HP), 1.0, 6.0, ((0, 64), (1, 4))),
        "w_in": gaussian(splits[4], (D, PROJ), D ** -0.5, 0.09375, ((0, 64),)),
        "a_log": jnp.clip(jax.random.uniform(splits[5], (H,), jnp.float32, -3.0, 0.7), -3.0, 0.7),
        "dt_bias": jnp.clip(jax.random.uniform(splits[6], (H,), jnp.float32, -5.0, -3.0), -5.0, -3.0),
        "d_skip": jnp.clip(jax.random.uniform(splits[7], (H,), jnp.float32, 0.5, 1.5), 0.5, 1.5),
    }


def span_forward(proj, xf, ids, a_log, dt_bias, d_skip, h_in):
    length = proj.shape[0]
    heads = a_log.shape[0]
    state = (proj.shape[1] - heads) // 2
    b_mat = proj[:, :state]
    c_mat = proj[:, state:2 * state]
    step = jax.nn.softplus(proj[:, 2 * state:] + dt_bias[None, :])
    cum = jnp.cumsum(-step * jnp.exp(a_log)[None, :], axis=0)
    order = jnp.arange(length)
    keep = (ids[:, None] == ids[None, :]) & (order[:, None] >= order[None, :])
    scores = jnp.dot(c_mat, b_mat.T, precision=lax.Precision.HIGHEST)
    gap = jnp.where(keep[None], cum.T[:, :, None] - cum.T[:, None, :], -1e+30)
    mixing = jnp.exp(gap) * scores[None] * step.T[:, None, :]
    xh = xf.reshape(length, heads, -1)
    intra = jnp.einsum('hts,shp->thp', mixing, xh, precision=lax.Precision.HIGHEST)
    lead = (ids == ids[0]).astype(jnp.float32)
    reach = lead[:, None] * jnp.exp(cum)
    carried = jnp.einsum('tn,hpn->thp', c_mat, h_in, precision=lax.Precision.HIGHEST)
    out = intra + reach[:, :, None] * carried + d_skip[None, :, None] * xh
    tail = (ids == ids[-1]).astype(jnp.float32)
    end_w = tail[:, None] * jnp.exp(cum[-1][None, :] - cum) * step
    s_end = jnp.einsum('thp,tn->hpn', xh * end_w[:, :, None], b_mat, precision=lax.Precision.HIGHEST)
    whole = (ids[0] == ids[-1]).astype(jnp.float32)
    h_out = s_end + (whole * jnp.exp(cum[-1]))[:, None, None] * h_in
    return (out.reshape(length, -1), h_out)

def sequence_forward(proj, xf, ids, a_log, dt_bias, d_skip):
    proj_c = proj.reshape(N_SEQ, TOK_DEV, proj.shape[1])
    x_c = xf.reshape(N_SEQ, TOK_DEV, xf.shape[1])
    id_c = ids.reshape(N_SEQ, TOK_DEV)

    def stepper(carry, block):
        state_now, last = carry
        p_b, x_b, i_b = block
        cont = (i_b[0] == last).astype(jnp.float32)
        y_b, h_out = span_forward(p_b, x_b, i_b, a_log, dt_bias, d_skip, cont * state_now)
        return ((h_out, i_b[-1]), y_b)
    init = (jnp.zeros((H, P_SIZE, N), jnp.float32), jnp.array(-1, jnp.int32))
    _, ys = lax.scan(stepper, init, (proj_c, x_c, id_c))
    return ys.reshape(xf.shape[0], -1)

def reference(layer_in, head_in, ids, dy, w_in, a_log, dt_bias, d_skip):

    def one(total, block):
        u_s, x_s, id_s, dy_s = block
        proj = jnp.dot(u_s, w_in, preferred_element_type=jnp.float32)
        xf = x_s.astype(jnp.float32)

        def forward(p_in, x_in):
            return sequence_forward(p_in, x_in, id_s, a_log, dt_bias, d_skip)
        y_s, pull = jax.vjp(forward, proj, xf)
        d_proj, d_x = pull(dy_s.astype(jnp.float32))
        d_round = d_proj.astype(jnp.bfloat16)
        d_u = jnp.dot(d_round, w_in.T, preferred_element_type=jnp.float32)
        total = total + lax.dot_general(u_s, d_round, (((0,), (0,)), ((), ())), preferred_element_type=jnp.float32)
        return (total, (y_s.astype(jnp.bfloat16), d_x.astype(jnp.bfloat16), d_u.astype(jnp.bfloat16)))
    zeros = jnp.zeros(w_in.shape, jnp.float32)
    total, outs = lax.scan(one, zeros, (layer_in, head_in, ids, dy))
    return (outs[0], outs[1], outs[2], total)
```

```python
import functools

import jax
import jax.numpy as jnp
from jax import lax
from jax.experimental import pallas as pl
from jax.experimental.pallas import tpu as pltpu
from jax.sharding import PartitionSpec as P

bf16, f32 = jnp.bfloat16, jnp.float32
NY, NZ, NC, NX = 4, 8, 2, 4
T, L, D, H, PS, N, PROJ = 256, 128, 4096, 64, 64, 128, 320
GL, GH = 512, 8
PL = 1024
VMEM = functools.partial(pl.BlockSpec, memory_space=pltpu.VMEM)
SMEM = functools.partial(pl.BlockSpec, memory_space=pltpu.SMEM)
PARAMS = pltpu.CompilerParams(vmem_limit_bytes=60 * 1024 * 1024)
SMALL = pltpu.CompilerParams(vmem_limit_bytes=20 * 1024 * 1024)
ANY = pl.BlockSpec(memory_space=pl.ANY)
HIGHEST = lax.Precision.HIGHEST
COST = pl.CostEstimate(flops=1 << 20, bytes_accessed=1 << 16, transcendentals=0)


def fetch(value, source):
    pairs = []
    for y in range(NY):
        for z in range(NZ):
            for c in range(NC):
                for x in range(NX):
                    sy, sz, sc, sx = source(y, z, c, x)
                    at = ((sy % NY * NZ + sz % NZ) * NC + sc % NC) * NX + sx % NX
                    pairs.append((at, ((y * NZ + z) * NC + c) * NX + x))
    return lax.ppermute(value, ("dp", "seq"), pairs)


def shift(value, dy=0, dz=0, dc=0, dx=0):
    return fetch(value, lambda y, z, c, x: (y + dy, z + dz, c + dc, x + dx))


def from_seq(value, offset):
    pairs = [(s + offset, s) for s in range(NX) if 0 <= s + offset < NX]
    return lax.ppermute(value, "seq", pairs)


def dot(a, b, dims=((1,), (0,)), precision=None):
    return lax.dot_general(
        a, b, (dims, ((), ())), preferred_element_type=f32, precision=precision
    )


def parts(value, count):
    out, rest = [], value
    for _ in range(count):
        piece = rest.astype(bf16)
        out.append(piece)
        rest = rest - piece.astype(f32)
    return out


def expand(value, ind, count=2):
    return sum(dot(piece, ind) for piece in parts(value, count))


def head_lanes(first_head, copies, lanes, shift_bits):
    rows = lax.broadcasted_iota(jnp.int32, (copies * H, lanes), 0)
    cols = lax.broadcasted_iota(jnp.int32, (copies * H, lanes), 1)
    return ((rows & (H - 1)) == (cols >> shift_bits) + first_head).astype(f32).astype(bf16)


def lanes_head(first_head, lanes):
    rows = lax.broadcasted_iota(jnp.int32, (lanes, H), 0)
    cols = lax.broadcasted_iota(jnp.int32, (lanes, H), 1)
    return (cols == (rows >> 6) + first_head).astype(f32).astype(bf16)


def put_parts(ref, value, count):
    width = value.shape[1]
    for i, piece in enumerate(parts(value, count)):
        ref[:, i * width : (i + 1) * width] = piece


ORDER = (7, 0, 1, 2, 3, 4, 5, 6)
PLAN = ((0, 0, 8), (1, 0, 8), (3, 0, 8), (2, 0, 4), (2, 4, 8))


def prep_kernel(pos, u, x_hbm, dy_hbm, idc, a_log, dt_bias, d_skip, *refs):
    pieces, outs = refs[:10], refs[10:]
    (w_abs, b_out, c_out, bb_out, cc_out, sig_out, stept_out, cumt_out,
     cum3, ew2, re2, cross2, vecs, s_end, g_in, link_out, linkn_out, x, dy, sems) = outs
    copies = [
        pltpu.make_async_copy(source, target, sems.at[i])
        for i, (source, target) in enumerate(((x_hbm, x), (dy_hbm, dy)))
    ]
    for copy in copies:
        copy.start()
    my_y, my_z, my_c = pos[0], pos[1], pos[2]
    for core in range(2):
        for (yo, lo, hi), piece in zip(PLAN, pieces[5 * core : 5 * core + 5]):
            for k in range(lo, hi):
                owner = (
                    lax.rem(my_y + yo, NY) * NZ + lax.rem(my_z + ORDER[k], NZ)
                ) * NC + lax.rem(my_c + core, NC)
                w_abs[pl.ds(pl.multiple_of(owner * 64, 64), 64), :] = piece[
                    (k - lo) * 64 : (k - lo + 1) * 64, :
                ]
    proj = dot(u[...], w_abs[...])
    b, c = proj[:, :N], proj[:, N : 2 * N]
    z = proj[:, 2 * N :] + dt_bias[...]
    small = jnp.exp(-jnp.abs(z))
    step = jnp.maximum(z, 0.0) + jnp.log1p(small)
    sig = jnp.where(z >= 0, 1.0, small) / (1.0 + small)
    sig_out[:, :H] = sig
    tiny = step < 1e-30
    sig_out[:, H:] = jnp.where(tiny, 1.0, sig / jnp.where(tiny, 1.0, step))
    la = -step * jnp.exp(a_log[...])
    rows = lax.broadcasted_iota(jnp.int32, (T, T), 0)
    cols = lax.broadcasted_iota(jnp.int32, (T, T), 1)
    tril = (rows >= cols).astype(f32).astype(bf16)
    cum = sum(dot(tril, piece) for piece in parts(la, 3))
    ids = idc[...]
    id0, idm, ide = ids[0:1], ids[L - 1 : L], ids[T - 1 : T]
    nxt, prv = pieces[3][256:257, 0:1].astype(f32), pieces[4][256:257, 0:1].astype(f32)
    link = jnp.where((prv == id0.astype(f32)) & (pos[3] > 0), 1.0, 0.0)
    linkn = jnp.where((nxt == ide.astype(f32)) & (pos[3] < NX - 1), 1.0, 0.0)
    link_out[...] = link
    linkn_out[...] = linkn
    cm, ce = cum[L - 1 : L], cum[T - 1 : T]
    reach = (ids == id0).astype(f32) * jnp.exp(cum)
    end_w = (ids == ide).astype(f32) * jnp.exp(ce - cum) * step
    put_parts(ew2, end_w, 2)
    put_parts(re2, reach, 2)
    a_end = (id0 == ide).astype(f32) * jnp.exp(ce)
    vec = jnp.concatenate(
        [a_end * link, a_end * linkn, a_end, d_skip[...]] * 2, axis=0
    )
    vec_parts = parts(vec, 3)
    put_parts(bb_out, b, 2)
    put_parts(cc_out, c, 2)
    bt = [piece.astype(bf16) for piece in parts(b.T, 2)]
    ct = [piece.astype(bf16) for piece in parts(c.T, 2)]
    for copy in copies:
        copy.wait()
    for g in range(H // GH):
        lanes = slice(g * GL, (g + 1) * GL)
        ind = head_lanes(g * GH, 2, GL, 6)
        xw = (x[:, lanes].astype(f32) * dot(ew2[...], ind)).astype(bf16)
        s_end[:, lanes] = (dot(bt[0], xw) + dot(bt[1], xw)).astype(bf16)
        dyr = (dy[:, lanes].astype(f32) * dot(re2[...], ind)).astype(bf16)
        g_in[:, lanes] = (dot(ct[0], dyr) + dot(ct[1], dyr)).astype(bf16)
        vecs[:, lanes] = sum(dot(piece, ind[:H]) for piece in vec_parts)
    b_out[...] = b
    c_out[...] = c
    stept_out[...] = step.T
    cumt_out[...] = cum.T
    put_parts(cum3, cum, 3)
    late = (ids[L:] == idm).astype(f32) * jnp.exp(cum[L:] - cm)
    early = (ids[:L] == idm).astype(f32) * jnp.exp(cm - cum[:L])
    put_parts(cross2, jnp.concatenate([early * step[:L], late], axis=0), 2)


def prep(pos, u, x, dy, idc, a_log, dt_bias, d_skip, pieces):
    def shape(rows, cols, kind=f32):
        return jax.ShapeDtypeStruct((rows, cols), kind)

    return pl.pallas_call(
        prep_kernel,
        out_shape=(
            shape(D, PROJ, bf16), shape(T, N), shape(T, N), shape(T, 2 * N, bf16),
            shape(T, 2 * N, bf16), shape(T, 2 * H), shape(H, T), shape(H, T),
            shape(T, 3 * H, bf16), shape(T, 2 * H, bf16), shape(T, 2 * H, bf16),
            shape(T, 2 * H, bf16), shape(8, D), shape(N, D, bf16), shape(N, D, bf16),
            shape(1, 1), shape(1, 1),
        ),
        in_specs=[SMEM(), VMEM()] + [pl.BlockSpec(memory_space=pl.ANY)] * 2
        + [VMEM()] * (4 + len(pieces)),
        out_specs=tuple([VMEM()] * 17),
        scratch_shapes=[
            pltpu.VMEM((T, D), bf16), pltpu.VMEM((T, D), bf16), pltpu.SemaphoreType.DMA((2,)),
        ],
        compiler_params=PARAMS,
        cost_estimate=COST,
    )(pos, u, x, dy, idc, a_log, dt_bias, d_skip, *pieces)


def intra_kernel(
    x, dy, cumt, stept, cum3, ew2, re2, cross2, b, c, bb, cc, idc, idr,
    y_out, dx_out, dyr_out, xw_out, d_out, row_out, col_out, ds_out, dbc_out, token, sc,
):
    g = pl.program_id(0)
    rows = lax.broadcasted_iota(jnp.int32, (L, L), 0)
    cols = lax.broadcasted_iota(jnp.int32, (L, L), 1)

    @pl.when(g == 0)
    def _():
        for k in range(2):
            span = slice(k * L, (k + 1) * L)
            scores = dot(c[span, :], b[span, :], ((1,), (1,)), HIGHEST)
            keep = (idc[span, :] == idr[:, span]) & (rows >= cols)
            sc[k] = jnp.where(keep, scores, 0.0)
        for out in (d_out, row_out, col_out, ds_out, dbc_out, token):
            out[...] = jnp.zeros_like(out)

    cum_e = dot(cum3[...], head_lanes(g * GH, 3, GH * L, 7))
    low = lax.broadcasted_iota(jnp.int32, (L, L), 1) < PS
    cumt_g, stept_g = cumt[...], stept[...]
    for k in range(2):
        span = slice(k * L, (k + 1) * L)
        total = jnp.zeros((L, L), f32)
        scores = sc[k]
        for q in range(GH // 2):
            lanes = slice(q * L, (q + 1) * L)
            dyp, xp = dy[span, lanes], x[span, lanes]
            zero = jnp.zeros_like(xp)
            xm = jnp.concatenate([jnp.where(low, xp, zero), jnp.where(low, zero, xp)], axis=0)
            dym = jnp.concatenate([jnp.where(low, dyp, zero), jnp.where(low, zero, dyp)], axis=0)
            grad = dot(dyp, xm, ((1,), (1,)))
            mixing = []
            for half in range(2):
                h = 2 * q + half
                gap = cum_e[span, h * L : (h + 1) * L] - cumt_g[h : h + 1, span]
                e = jnp.exp(jnp.minimum(gap, 0.0)) * stept_g[h : h + 1, span]
                total += e * grad[:, half * L : (half + 1) * L]
                mixing.append((e * scores).astype(bf16))
            y_out[span, lanes] = dot(jnp.concatenate(mixing, axis=1), xm)
            dx_out[span, lanes] = dot(jnp.concatenate(mixing, axis=0), dym, ((0,), (0,)))
        ds_out[k] += total
    ind = head_lanes(g * GH, 2, GL, 6)
    pool = lanes_head(g * GH, GL)

    def pooled(value):
        return sum(dot(piece, pool) for piece in parts(value, 2))

    xf, dyf = x[...].astype(f32), dy[...].astype(f32)
    cross = dot(cross2[...], ind)
    xw = (xf[:L] * cross[:L]).astype(bf16)
    dyr = (dyf[L:] * cross[L:]).astype(bf16)
    state = sum(dot(piece, xw) for piece in parts(b[:L, :].T, 2)).astype(bf16)
    back = sum(dot(piece, dyr) for piece in parts(c[L:, :].T, 2)).astype(bf16)
    last = ((1,), (1,))
    dbc_out[0] += dot(xw, back, last)
    dbc_out[1] += dot(dyr, state, last)
    read = dot(cc[L:, :], twice(state))
    sent = dot(bb[:L, :], twice(back))
    row_out[L:, :] += pooled(dyr.astype(f32) * read)
    far = pooled(xw.astype(f32) * sent)
    col = xf * dx_out[...]
    near = pooled(col)
    d_out[...] += near - pooled(dyf * y_out[...])
    d_out[:L, :] += far
    col_out[...] += near
    col_out[:L, :] += far
    y_out[L:, :] += cross[L:] * read
    dx_out[:L, :] += cross[:L] * sent
    xw_out[...] = (xf * dot(ew2[...], ind)).astype(bf16)
    dyr_out[...] = (dyf * dot(re2[...], ind)).astype(bf16)


def whole(*dims):
    return VMEM(dims, lambda i: (0,) * len(dims))


def block(rows, lanes=GL):
    return VMEM((rows, lanes), lambda i: (0, i))


def twice(value):
    return jnp.concatenate([value, value], axis=0)


def intra(x, dy, cumt, stept, cum3, ew2, re2, cross2, b, c, bb, cc, idc, idr):
    def shape(*dims, kind=f32):
        return jax.ShapeDtypeStruct(dims, kind)

    heads = VMEM((GH, T), lambda i: (i, 0))
    return pl.pallas_call(
        intra_kernel,
        grid=(H // GH,),
        out_shape=(
            shape(T, D), shape(T, D), shape(T, D, kind=bf16), shape(T, D, kind=bf16),
            shape(T, H), shape(T, H), shape(T, H), shape(2, L, L), shape(2, L, N), shape(8, 128),
        ),
        in_specs=[
            block(T), block(T), heads, heads, whole(T, 3 * H), whole(T, 2 * H),
            whole(T, 2 * H), whole(T, 2 * H), whole(T, N), whole(T, N), whole(T, 2 * N),
            whole(T, 2 * N), whole(T, 1), whole(1, T),
        ],
        out_specs=(
            block(T), block(T), block(T), block(T), whole(T, H), whole(T, H), whole(T, H),
            whole(2, L, L), whole(2, L, N), whole(8, 128),
        ),
        scratch_shapes=[pltpu.VMEM((2, L, L), f32)],
        compiler_params=PARAMS,
        cost_estimate=COST,
    )(x, dy, cumt, stept, cum3, ew2, re2, cross2, b, c, bb, cc, idc, idr)


def hop_kernel(one, back, vecs, token, out_one, out_back):
    out_one[...] = (one[...].astype(f32) * vecs[0:1, :]).astype(bf16)
    out_back[...] = (back[...].astype(f32) * vecs[1:2, :]).astype(bf16)


def hop(one, back, vecs, token):
    return pl.pallas_call(
        hop_kernel,
        grid=(D // PL,),
        out_shape=(jax.ShapeDtypeStruct((N, D), bf16),) * 2,
        in_specs=[block(N, PL), block(N, PL), block(8, PL), ANY],
        out_specs=(block(N, PL),) * 2,
        compiler_params=SMALL,
        cost_estimate=COST,
    )(one, back, vecs, token)


def arrived(one, two, link):
    return (link[...] * (one[...].astype(f32) + two[...].astype(f32))).astype(bf16)


def post_kernel(
    r1, r2, b1, b2, dyr, xw, vecs, bb, cc, link, linkn,
    d, row_in, col_in, ds, dbc, sig, b, c, idc, idr, a_log, dround, dlow,
    dc_acc, db_acc, row_acc, col_acc, flow_acc,
):
    g = pl.program_id(0)

    @pl.when(g == 0)
    def _():
        for acc in (dc_acc, db_acc, row_acc, col_acc, flow_acc):
            acc[...] = jnp.zeros_like(acc)

    pool = lanes_head(g * (PL // PS), PL)
    s0, dse = arrived(r1, r2, link), arrived(b1, b2, linkn)
    last = ((1,), (1,))
    dc_acc[...] += dot(dyr[...], s0, last)
    db_acc[...] += dot(xw[...], dse, last)
    read, sent = dot(cc[:, :N], s0), dot(bb[:, :N], dse)
    row_acc[...] += dot((dyr[...].astype(f32) * read).astype(bf16), pool)
    col_acc[...] += dot((xw[...].astype(f32) * sent).astype(bf16), pool)
    flow = vecs[2:3, :] * jnp.sum(s0.astype(f32) * dse.astype(f32), axis=0, keepdims=True)
    flow_acc[...] += sum(dot(piece, pool) for piece in parts(flow, 2))


    @pl.when(g == pl.num_programs(0) - 1)
    def _():
        close(
            dc_acc, db_acc, row_acc, col_acc, flow_acc, d, row_in, col_in, ds, dbc, sig, b, c,
            idc, idr, a_log, dround, dlow,
        )


def close(
    dc, db, row, col, flow, d, row_in, col_in, ds, dbc, sig, b, c, idc, idr, a_log, dround, dlow
):
    rows = lax.broadcasted_iota(jnp.int32, (T, T), 0)
    cols = lax.broadcasted_iota(jnp.int32, (T, T), 1)
    same = (rows >> 7) == (cols >> 7)

    def mask(value):
        return value.astype(f32).astype(bf16)

    def total(where, value, count):
        return sum(dot(mask(where), piece) for piece in parts(value, count))

    dla = total(same & (rows > cols), d[...], 3) + total(same & (rows <= cols), row_in[...], 3)
    dla += total(rows > cols, col[...], 3) + total(rows <= cols, row[...], 3) + flow[...]

    def put(span, lanes, value):
        dround[span, lanes] = value.astype(bf16)
        dlow[span, lanes] = (value - value.astype(bf16).astype(f32)).astype(bf16)

    direct = (col_in[...] + col[...]) * sig[:, H:]
    put(slice(0, T), slice(2 * N, PROJ), direct - dla * jnp.exp(a_log[...]) * sig[:, :H])
    rows = lax.broadcasted_iota(jnp.int32, (L, L), 0)
    cols = lax.broadcasted_iota(jnp.int32, (L, L), 1)
    for k in range(2):
        span = slice(k * L, (k + 1) * L)
        keep = (idc[span, :] == idr[:, span]) & (rows >= cols)
        kept = jnp.where(keep, ds[k], 0.0)
        to_b = dot(kept, c[span, :], ((0,), (0,)), HIGHEST) + db[span, :]
        to_c = dot(kept, b[span, :], precision=HIGHEST) + dc[span, :]
        if k == 0:
            to_b += dbc[0]
        else:
            to_c += dbc[1]
        put(span, slice(0, N), to_b)
        put(span, slice(N, 2 * N), to_c)


def post(*args):
    def lanes(rows):
        return block(rows, PL)

    return pl.pallas_call(
        post_kernel,
        grid=(D // PL,),
        out_shape=(jax.ShapeDtypeStruct((T, PROJ), bf16), jax.ShapeDtypeStruct((T, PROJ), bf16)),
        in_specs=[lanes(N)] * 4 + [lanes(T)] * 2 + [
            lanes(8), whole(T, 2 * N), whole(T, 2 * N), whole(1, 1), whole(1, 1),
            whole(T, H), whole(T, H), whole(T, H), whole(2, L, L), whole(2, L, N),
            whole(T, 2 * H), whole(T, N), whole(T, N), whole(T, 1), whole(1, T), whole(1, H),
        ],
        out_specs=(whole(T, PROJ), whole(T, PROJ)),
        scratch_shapes=[
            pltpu.VMEM((T, N), f32), pltpu.VMEM((T, N), f32), pltpu.VMEM((T, H), f32),
            pltpu.VMEM((T, H), f32), pltpu.VMEM((1, H), f32),
        ],
        compiler_params=SMALL,
        cost_estimate=COST,
    )(*args)


def gradw_kernel(pos, ua, ub, da, db, g0, g1, g3, g2a, g2b):
    my_y, my_z = pos[0], pos[1]
    for out, (yo, lo, hi) in zip((g0, g1, g3, g2a, g2b), PLAN):
        for k in range(lo, hi):
            chip = lax.rem(my_y + yo, NY) * NZ + lax.rem(my_z + ORDER[k], NZ)
            at = pl.ds(pl.multiple_of(chip * 64, 64), 64)
            rows = dot(ua[at, :], da[...]) + dot(ub[at, :], db[...])
            out[(k - lo) * 64 : (k - lo + 1) * 64, :] = rows.astype(out.dtype)


def gradw(pos, ua, ub, da, db):
    def shape(rows, kind=bf16):
        return jax.ShapeDtypeStruct((rows, PROJ), kind)

    return pl.pallas_call(
        gradw_kernel,
        out_shape=(shape(512, f32), shape(512), shape(512), shape(256), shape(256)),
        in_specs=[SMEM()] + [VMEM()] * 4,
        out_specs=tuple([VMEM()] * 5),
        compiler_params=SMALL,
        cost_estimate=COST,
    )(pos, ua, ub, da, db)


def gradu_kernel(dhi, dlo, w, out_u, token):
    token[...] = jnp.zeros_like(token)
    last = ((1,), (1,))
    out_u[...] = (dot(dhi[...], w[...], last) + dot(dlo[...], w[...], last)).astype(bf16)


def gradu(dhi, dlo, w):
    return pl.pallas_call(
        gradu_kernel,
        grid=(D // PL,),
        out_shape=(jax.ShapeDtypeStruct((T, D), bf16), jax.ShapeDtypeStruct((8, 128), f32)),
        in_specs=[whole(T, PROJ), whole(T, PROJ), VMEM((PL, PROJ), lambda i: (i, 0))],
        out_specs=(block(T, PL), whole(8, 128)),
        compiler_params=SMALL,
        cost_estimate=COST,
    )(dhi, dlo, w)


def finish_kernel(
    r1, r2, b1, b2, vecs, bb, cc, link, linkn, x, dy, y, dx, ew2, re2, after, out_y, out_x, token
):
    token[...] = jnp.zeros_like(token)
    ind = head_lanes(pl.program_id(0) * GH, 2, GL, 6)
    s0, dse = arrived(r1, r2, link), arrived(b1, b2, linkn)
    skip = vecs[3:4, :]
    y_off = dot(re2[...], ind) * dot(cc[...], twice(s0))
    out_y[...] = (y[...] + y_off + skip * x[...].astype(f32)).astype(bf16)
    dx_off = dot(ew2[...], ind) * dot(bb[...], twice(dse))
    out_x[...] = (dx[...] + dx_off + skip * dy[...].astype(f32)).astype(bf16)


def finish(*args):
    shape = jax.ShapeDtypeStruct((T, D), bf16)
    return pl.pallas_call(
        finish_kernel,
        grid=(H // GH,),
        out_shape=(shape,) * 2 + (jax.ShapeDtypeStruct((8, 128), f32),),
        in_specs=[block(N)] * 4 + [
            block(8), whole(T, 2 * N), whole(T, 2 * N), whole(1, 1), whole(1, 1),
            block(T), block(T), block(T), block(T), whole(T, 2 * H), whole(T, 2 * H), ANY,
        ],
        out_specs=(block(T),) * 2 + (whole(8, 128),),
        compiler_params=SMALL,
        cost_estimate=COST,
    )(*args)


def sum_y_kernel(own, up, down, far_a, far_b, token, near, out_up, out_down):
    total = own[...] + up[...].astype(f32) + down[...].astype(f32)
    total += jnp.concatenate([far_a[...], far_b[...]], axis=0).astype(f32)
    near[...] = total[:192]
    out_up[...] = total[192:384].astype(bf16)
    out_down[...] = total[384:].astype(bf16)


def sum_z_kernel(near, up, down, token, here, left, right):
    left[...] = (near[:64] + up[:64].astype(f32)).astype(bf16)
    here[...] = near[64:128] + up[64:128].astype(f32) + down[:64].astype(f32)
    right[...] = (near[128:] + up[128:].astype(f32) + down[64:].astype(f32)).astype(bf16)


def sums(kernel, outs, args, token):
    return pl.pallas_call(
        kernel,
        out_shape=tuple(jax.ShapeDtypeStruct((rows, PROJ), kind) for rows, kind in outs),
        in_specs=[VMEM()] * len(args) + [ANY],
        out_specs=tuple([VMEM()] * len(outs)),
        compiler_params=SMALL,
        cost_estimate=COST,
    )(*args, token)


def body(layer_in, head_in, ids, dy, w_in, a_log, dt_bias, d_skip):
    u, x, dyv = layer_in[0], head_in[0], dy[0]
    dp, seq = lax.axis_index("dp"), lax.axis_index("seq")
    my_y = (dp // (NZ * NC) + 2 * (seq % 2)) % NY
    pos = jnp.stack([my_y, (dp // NC) % NZ, dp % NC, seq]).astype(jnp.int32)
    idc, idr = ids.reshape(T, 1), ids.reshape(1, T)
    a_log, dt_bias, d_skip = (v.reshape(1, H) for v in (a_log, dt_bias, d_skip))

    def start(k):
        return fetch(w_in, lambda y, z, c, x: (y + 2 * (x % 2), z + k, c, x))

    near = [start(-1), start(0), start(1)]
    near, u, pos, idc = lax.optimization_barrier((near, u, pos, idc))
    near = jnp.concatenate(near, axis=0)
    high, low = shift(near, dz=3), shift(near[64:], dz=-3)

    split = u.reshape(T, NY * NZ, NC, 64)
    mine = lax.dynamic_index_in_dim(split, pos[2], 2, False)
    other = lax.dynamic_index_in_dim(split, 1 - pos[2], 2, False)
    ua = mine.transpose(1, 2, 0).reshape(D // 2, T)
    ub = shift(other.transpose(1, 2, 0).reshape(D // 2, T), dc=1)

    high, low, ua, ub = lax.optimization_barrier((high, low, ua, ub))
    row = jnp.concatenate([near, high, low], axis=0)
    up, down = shift(row, dy=1), shift(row, dy=-1)

    def with_id(rows, number):
        edge = jnp.broadcast_to(number.reshape(1, 1).astype(bf16), (16, PROJ))
        return jnp.concatenate([rows, edge], axis=0)

    far_a = shift(with_id(row[:256], ids[0, 0]), dx=1)
    far_b = shift(with_id(row[256:], ids[0, -1]), dx=-1)
    own = [row, up, down, far_a, far_b]
    pieces = own + [shift(piece[:512] if i < 3 else piece, dc=1) for i, piece in enumerate(own)]

    (w_abs, b, c, bb, cc, sig, stept, cumt, cum3, ew2, re2, cross2, vecs, s_end, g_in, link,
     linkn) = prep(pos, u, x, dyv, idc, a_log, dt_bias, d_skip, pieces)

    r1, b1 = from_seq(s_end, -1), from_seq(g_in, 1)
    y_in, dx_in, dyr, xw, d, row_in, col_in, ds, dbc, token = intra(
        x, dyv, cumt, stept, cum3, ew2, re2, cross2, b, c, bb, cc, idc, idr
    )
    m1, n1 = hop(r1, b1, vecs, token)
    r2, b2 = from_seq(m1, -1), from_seq(n1, 1)
    got = (r1, r2, b1, b2)
    shared = (vecs, bb, cc, link, linkn)
    dround, dlow = post(
        *got, dyr, xw, *shared, d, row_in, col_in, ds, dbc, sig, b, c, idc, idr, a_log
    )
    dother = shift(dround, dc=1)
    g0, g1, g3, g2a, g2b = gradw(pos, ua, ub, dround, dother)
    parts_y = (
        g0, shift(g1, dy=-1), shift(g3, dy=1), shift(g2a, dx=-1), shift(g2b, dx=1)
    )
    out_u, token = gradu(dround, dlow, w_abs)
    near, up, down = sums(sum_y_kernel, ((192, f32), (192, bf16), (128, bf16)), parts_y, token)
    up, down = shift(up, dz=-3), shift(down, dz=3)
    out_y, out_x, token = finish(*got, *shared, x, dyv, y_in, dx_in, ew2, re2, token)
    here, left, right = sums(
        sum_z_kernel, ((64, f32), (64, bf16), (64, bf16)), (near, up, down), token
    )
    part = here + shift(right, dz=-1).astype(f32) + shift(left, dz=1).astype(f32)
    grad_w = sum(
        fetch(part, lambda y, z, c, x, k=k: (y + 2 * ((x + k) % 2), z, c, x + k))
        for k in range(NX)
    )
    return out_y[None], out_x[None], out_u[None], grad_w


def solution(mesh):
    return jax.shard_map(
        body,
        mesh=mesh,
        in_specs=(
            P("dp", "seq", None), P("dp", "seq", None), P("dp", "seq"), P("dp", "seq", None),
            P("dp", None), P(), P(), P(),
        ),
        out_specs=(P("dp", "seq", None), P("dp", "seq", None), P("dp", "seq", None), P("dp", None)),
        check_vma=False,
    )
```

```python
import functools

import jax
import jax.numpy as jnp
from jax import lax
from jax.experimental import pallas as pl
from jax.experimental.pallas import tpu as pltpu
from jax.sharding import PartitionSpec as P

bf16, f32 = jnp.bfloat16, jnp.float32
NY, NZ, NC, NX = 4, 8, 2, 4
T, L, D, H, PS, N, PROJ = 256, 128, 4096, 64, 64, 128, 320
GL, GH = 512, 8
PL = 1024
HALF = D // 2
VMEM = functools.partial(pl.BlockSpec, memory_space=pltpu.VMEM)
SMEM = functools.partial(pl.BlockSpec, memory_space=pltpu.SMEM)
PARAMS = pltpu.CompilerParams(vmem_limit_bytes=60 * 1024 * 1024)
SMALL = pltpu.CompilerParams(vmem_limit_bytes=20 * 1024 * 1024)
ANY = pl.BlockSpec(memory_space=pl.ANY)
HIGHEST = lax.Precision.HIGHEST
COST = pl.CostEstimate(flops=1 << 20, bytes_accessed=1 << 16, transcendentals=0)


def fetch(value, source):
    pairs = []
    for y in range(NY):
        for z in range(NZ):
            for c in range(NC):
                for x in range(NX):
                    sy, sz, sc, sx = source(y, z, c, x)
                    at = ((sy % NY * NZ + sz % NZ) * NC + sc % NC) * NX + sx % NX
                    pairs.append((at, ((y * NZ + z) * NC + c) * NX + x))
    return lax.ppermute(value, ("dp", "seq"), pairs)


def shift(value, dy=0, dz=0, dc=0, dx=0):
    return fetch(value, lambda y, z, c, x: (y + dy, z + dz, c + dc, x + dx))


def from_seq(value, offset):
    pairs = [(s + offset, s) for s in range(NX) if 0 <= s + offset < NX]
    return lax.ppermute(value, "seq", pairs)


def dot(a, b, dims=((1,), (0,)), precision=None):
    return lax.dot_general(
        a, b, (dims, ((), ())), preferred_element_type=f32, precision=precision
    )


def parts(value, count):
    out, rest = [], value
    for _ in range(count):
        piece = rest.astype(bf16)
        out.append(piece)
        rest = rest - piece.astype(f32)
    return out


def expand(value, ind, count=2):
    return sum(dot(piece, ind) for piece in parts(value, count))


def head_lanes(first_head, copies, lanes, shift_bits):
    rows = lax.broadcasted_iota(jnp.int32, (copies * H, lanes), 0)
    cols = lax.broadcasted_iota(jnp.int32, (copies * H, lanes), 1)
    return ((rows & (H - 1)) == (cols >> shift_bits) + first_head).astype(f32).astype(bf16)


def lanes_head(first_head, lanes):
    rows = lax.broadcasted_iota(jnp.int32, (lanes, H), 0)
    cols = lax.broadcasted_iota(jnp.int32, (lanes, H), 1)
    return (cols == (rows >> 6) + first_head).astype(f32).astype(bf16)


def put_parts(ref, value, count):
    width = value.shape[1]
    for i, piece in enumerate(parts(value, count)):
        ref[:, i * width : (i + 1) * width] = piece


ORDER = (7, 0, 1, 2, 3, 4, 5, 6)
PLAN = ((0, 0, 8), (1, 0, 8), (3, 0, 8), (2, 0, 4), (2, 4, 8))


def assemble(pos, pieces, w):
    for core in range(2):
        for (yo, lo, hi), piece in zip(PLAN, pieces[5 * core : 5 * core + 5]):
            for k in range(lo, hi):
                owner = (
                    lax.rem(pos[0] + yo, NY) * NZ + lax.rem(pos[1] + ORDER[k], NZ)
                ) * NC + lax.rem(pos[2] + core, NC)
                w[pl.ds(pl.multiple_of(owner * 64, 64), 64), :] = piece[
                    (k - lo) * 64 : (k - lo + 1) * 64, :
                ]


def prep_kernel(pos, u, x_hbm, dy_hbm, idr, a_log, dt_bias, d_skip, *refs):
    pieces, outs = refs[:10], refs[10:]
    (b_out, c_out, bb_out, cc_out, sig_out, stept_out, cumt_out,
     cum3, ew2, re2, cross2, vecs, s_a, s_b, g_a, g_b, flags, idc, w_abs, x, dy, sems) = outs
    copies = [
        pltpu.make_async_copy(source, target, sems.at[i])
        for i, (source, target) in enumerate(((x_hbm, x), (dy_hbm, dy)))
    ]
    for copy in copies:
        copy.start()
    assemble(pos, pieces, w_abs)
    proj = dot(u[...], w_abs[...])
    b, c = proj[:, :N], proj[:, N : 2 * N]
    z = proj[:, 2 * N :] + dt_bias[...]
    small = jnp.exp(-jnp.abs(z))
    step = jnp.maximum(z, 0.0) + jnp.log1p(small)
    sig = jnp.where(z >= 0, 1.0, small) / (1.0 + small)
    sig_out[:, :H] = sig
    tiny = step < 1e-30
    sig_out[:, H:] = jnp.where(tiny, 1.0, sig / jnp.where(tiny, 1.0, step))
    la = -step * jnp.exp(a_log[...])
    rows = lax.broadcasted_iota(jnp.int32, (T, T), 0)
    cols = lax.broadcasted_iota(jnp.int32, (T, T), 1)
    tril = (rows >= cols).astype(f32).astype(bf16)
    cum = sum(dot(tril, piece) for piece in parts(la, 3))
    ids = jnp.broadcast_to(idr[...].astype(f32), (8, T)).T[:, 0:1]
    idc[...] = ids
    id0, idm, ide = ids[0:1], ids[L - 1 : L], ids[T - 1 : T]
    edge = slice(256, 257)
    link = (pieces[4][edge, 1:2].astype(f32) == id0) & (pos[3] > 0)
    linkn = (pieces[3][edge, 0:1].astype(f32) == ide) & (pos[3] < NX - 1)
    link, linkn = jnp.where(link, 1.0, 0.0), jnp.where(linkn, 1.0, 0.0)
    alone = [
        jnp.where(first == final, 1.0, 0.0)
        for first, final in ((id0, ide), *((p[edge, 0:1], p[edge, 1:2]) for p in (pieces[4], pieces[3])))
    ]
    flags[...] = jnp.concatenate([link, linkn] + alone + [link] * 3, axis=0)
    cm, ce = cum[L - 1 : L], cum[T - 1 : T]
    reach = (ids == id0).astype(f32) * jnp.exp(cum)
    end_w = (ids == ide).astype(f32) * jnp.exp(ce - cum) * step
    put_parts(ew2, end_w, 2)
    put_parts(re2, reach, 2)
    a_end = (id0 == ide).astype(f32) * jnp.exp(ce)
    vec = jnp.concatenate(
        [a_end * link, a_end * linkn, a_end, d_skip[...]] * 2, axis=0
    )
    vec_parts = parts(vec, 3)
    put_parts(bb_out, b, 2)
    put_parts(cc_out, c, 2)
    bt = [piece.astype(bf16) for piece in parts(b.T, 2)]
    ct = [piece.astype(bf16) for piece in parts(c.T, 2)]
    for copy in copies:
        copy.wait()
    for g in range(H // GH):
        lanes = slice(g * GL, (g + 1) * GL)
        ind = head_lanes(g * GH, 2, GL, 6)
        xw = (x[:, lanes].astype(f32) * dot(ew2[...], ind)).astype(bf16)
        s_end, g_in = (s_a, g_a) if g < 4 else (s_b, g_b)
        half = slice(g % 4 * GL, (g % 4 + 1) * GL)
        s_end[:, half] = (dot(bt[0], xw) + dot(bt[1], xw)).astype(bf16)
        dyr = (dy[:, lanes].astype(f32) * dot(re2[...], ind)).astype(bf16)
        g_in[:, half] = (dot(ct[0], dyr) + dot(ct[1], dyr)).astype(bf16)
        vecs[:, lanes] = sum(dot(piece, ind[:H]) for piece in vec_parts)
    b_out[...] = b
    c_out[...] = c
    stept_out[...] = step.T
    cumt_out[...] = cum.T
    put_parts(cum3, cum, 3)
    late = (ids[L:] == idm).astype(f32) * jnp.exp(cum[L:] - cm)
    early = (ids[:L] == idm).astype(f32) * jnp.exp(cm - cum[:L])
    put_parts(cross2, jnp.concatenate([early * step[:L], late], axis=0), 2)


def prep(pos, u, x, dy, idr, a_log, dt_bias, d_skip, pieces):
    def shape(rows, cols, kind=f32):
        return jax.ShapeDtypeStruct((rows, cols), kind)

    return pl.pallas_call(
        prep_kernel,
        out_shape=(
            shape(T, N), shape(T, N), shape(T, 2 * N, bf16), shape(T, 2 * N, bf16),
            shape(T, 2 * H), shape(H, T), shape(H, T),
            shape(T, 3 * H, bf16), shape(T, 2 * H, bf16), shape(T, 2 * H, bf16),
            shape(T, 2 * H, bf16), shape(8, D), *(shape(N, HALF, bf16) for _ in range(4)),
            shape(8, 1), shape(T, 1),
        ),
        in_specs=[SMEM(), VMEM()] + [pl.BlockSpec(memory_space=pl.ANY)] * 2
        + [VMEM()] * (4 + len(pieces)),
        out_specs=tuple([VMEM()] * 18),
        scratch_shapes=[
            pltpu.VMEM((D, PROJ), bf16), pltpu.VMEM((T, D), bf16), pltpu.VMEM((T, D), bf16),
            pltpu.SemaphoreType.DMA((2,)),
        ],
        compiler_params=PARAMS,
        cost_estimate=COST,
    )(pos, u, x, dy, idr, a_log, dt_bias, d_skip, *pieces)


def intra_kernel(
    start, x, dy, cumt, stept, cum3, ew2, re2, cross2, b, c, bb, cc, idc, idr, flags, *refs
):
    y_low, dx_low, dyr_out, xw_out, sums_out, ds_out, flags_out, sc, y_out, dx_out = refs[-10:]
    turn = pl.program_id(0)
    g = turn + start
    rows = lax.broadcasted_iota(jnp.int32, (L, L), 0)
    cols = lax.broadcasted_iota(jnp.int32, (L, L), 1)

    @pl.when(turn == 0)
    def _():
        for k in range(2):
            span = slice(k * L, (k + 1) * L)
            scores = dot(c[span, :], b[span, :], ((1,), (1,)), HIGHEST)
            keep = (idc[span, :] == idr[:, span].astype(f32)) & (rows >= cols)
            sc[k] = jnp.where(keep, scores, 0.0)
        flags_out[...] = flags[...]
        for out, before in zip((sums_out, ds_out), refs[:2]):
            out[...] = before[...] if start else jnp.zeros_like(out)

    cum_e = dot(cum3[...], head_lanes(g * GH, 3, GH * L, 7))
    low = lax.broadcasted_iota(jnp.int32, (L, L), 1) < PS
    cumt_g, stept_g = cumt[...], stept[...]
    for k in range(2):
        span = slice(k * L, (k + 1) * L)
        total = jnp.zeros((L, L), f32)
        scores = sc[k]
        for q in range(GH // 2):
            lanes = slice(q * L, (q + 1) * L)
            dyp, xp = dy[span, lanes], x[span, lanes]
            zero = jnp.zeros_like(xp)
            xm = jnp.concatenate([jnp.where(low, xp, zero), jnp.where(low, zero, xp)], axis=0)
            dym = jnp.concatenate([jnp.where(low, dyp, zero), jnp.where(low, zero, dyp)], axis=0)
            grad = dot(dyp, xm, ((1,), (1,)))
            mixing = []
            for half in range(2):
                h = 2 * q + half
                gap = cum_e[span, h * L : (h + 1) * L] - cumt_g[h : h + 1, span]
                e = jnp.exp(jnp.minimum(gap, 0.0)) * stept_g[h : h + 1, span]
                total += e * grad[:, half * L : (half + 1) * L]
                mixing.append((e * scores).astype(bf16))
            y_out[span, lanes] = dot(jnp.concatenate(mixing, axis=1), xm)
            dx_out[span, lanes] = dot(jnp.concatenate(mixing, axis=0), dym, ((0,), (0,)))
        ds_out[k, :, :L] += total
    ind = head_lanes(g * GH, 2, GL, 6)
    pool = lanes_head(g * GH, GL)

    def pooled(value):
        return sum(dot(piece, pool) for piece in parts(value, 2))

    xf, dyf = x[...].astype(f32), dy[...].astype(f32)
    cross = dot(cross2[...], ind)
    xw = (xf[:L] * cross[:L]).astype(bf16)
    dyr = (dyf[L:] * cross[L:]).astype(bf16)
    state = sum(dot(piece, xw) for piece in parts(b[:L, :].T, 2)).astype(bf16)
    back = sum(dot(piece, dyr) for piece in parts(c[L:, :].T, 2)).astype(bf16)
    last = ((1,), (1,))
    ds_out[0, :, L:] += dot(xw, back, last)
    ds_out[1, :, L:] += dot(dyr, state, last)
    read = dot(cc[L:, :], twice(state))
    sent = dot(bb[:L, :], twice(back))
    sums_out[L:, H : 2 * H] += pooled(dyr.astype(f32) * read)
    far = pooled(xw.astype(f32) * sent)
    col = xf * dx_out[...]
    near = pooled(col)
    sums_out[:, :H] += near - pooled(dyf * y_out[...])
    sums_out[:L, :H] += far
    sums_out[:, 2 * H :] += near
    sums_out[:L, 2 * H :] += far
    y_out[L:, :] += cross[L:] * read
    dx_out[:L, :] += cross[:L] * sent
    y_low[...] = y_out[...].astype(bf16)
    dx_low[...] = dx_out[...].astype(bf16)
    xw_out[...] = (xf * dot(ew2[...], ind)).astype(bf16)
    dyr_out[...] = (dyf * dot(re2[...], ind)).astype(bf16)


def whole(*dims):
    return VMEM(dims, lambda i: (0,) * len(dims))


def block(rows, lanes=GL, start=0):
    return VMEM((rows, lanes), lambda i: (0, i + start))


def twice(value):
    return jnp.concatenate([value, value], axis=0)


def intra(start, count, before, x, dy, cumt, stept, cum3, ew2, re2, cross2, b, c, bb, cc, idc,
          idr, flags):
    def shape(*dims, kind=f32):
        return jax.ShapeDtypeStruct(dims, kind)

    heads = VMEM((GH, T), lambda i: (i + start, 0))
    wide = block(T, GL, start)
    return pl.pallas_call(
        functools.partial(intra_kernel, start),
        grid=(count,),
        out_shape=(
            *(shape(T, D, kind=bf16) for _ in range(4)),
            shape(T, 3 * H), shape(2, L, L + N), shape(8, 1),
        ),
        in_specs=[
            wide, wide, heads, heads, whole(T, 3 * H), whole(T, 2 * H),
            whole(T, 2 * H), whole(T, 2 * H), whole(T, N), whole(T, N), whole(T, 2 * N),
            whole(T, 2 * N), whole(T, 1), whole(1, T), whole(8, 1),
        ] + ([whole(T, 3 * H), whole(2, L, L + N)] + [ANY] * 4 if start else []),
        out_specs=(wide, wide, wide, wide, whole(T, 3 * H), whole(2, L, L + N), whole(8, 1)),
        scratch_shapes=[
            pltpu.VMEM((2, L, L), f32), pltpu.VMEM((T, GL), f32), pltpu.VMEM((T, GL), f32)
        ],
        input_output_aliases={17 + i: i for i in range(4)} if start else {},
        compiler_params=PARAMS,
        cost_estimate=COST,
    )(x, dy, cumt, stept, cum3, ew2, re2, cross2, b, c, bb, cc, idc, idr, flags,
      *before[4:6], *before[:4])


def relay_kernel(turn, s_a, s_b, g_a, g_b, got_s, got_g, vecs, flags, out_s, out_g):
    later = flags[2:3, :] > 0.5
    lanes = slice(turn * HALF, (turn + 1) * HALF)
    for own, last, got, row, out in (
        (s_b if turn else s_a, s_b, got_s, 0, out_s), (g_b if turn else g_a, g_b, got_g, 1, out_g)
    ):
        on = own[...].astype(f32) + vecs[row : row + 1, lanes] * got[...].astype(f32)
        out[...] = jnp.where(later, on, last[...].astype(f32)).astype(bf16)


def relay(turn, *args):
    return pl.pallas_call(
        functools.partial(relay_kernel, turn),
        out_shape=(jax.ShapeDtypeStruct((N, HALF), bf16),) * 2,
        in_specs=[VMEM()] * 8,
        out_specs=(VMEM(), VMEM()),
        compiler_params=SMALL,
        cost_estimate=COST,
    )(*args)


def arrived(early, late, flags, side):
    one, two = early[...].astype(f32), late[...].astype(f32)
    value = jnp.where(flags[3 + side : 4 + side, :] > 0.5, two, one)
    return (flags[side : side + 1, :] * value).astype(bf16)


def post_kernel(
    half, r1, r2, b1, b2, dyr, xw, vecs, bb, cc, flags, *refs
):
    dc_acc, db_acc, sum_acc, flow_acc = refs[-4:]
    g = pl.program_id(0)

    @pl.when(g == 0)
    def _():
        for acc, before in zip(refs[-4:], refs[:4]):
            acc[...] = before[...] if half else jnp.zeros_like(acc)

    pool = lanes_head((half * (HALF // PL) + g) * (PL // PS), PL)
    s0, dse = arrived(r1, r2, flags, 0), arrived(b1, b2, flags, 1)
    last = ((1,), (1,))
    dc_acc[...] += dot(dyr[...], s0, last)
    db_acc[...] += dot(xw[...], dse, last)
    read, sent = dot(cc[:, :N], s0), dot(bb[:, :N], dse)
    sum_acc[:, :H] += dot((dyr[...].astype(f32) * read).astype(bf16), pool)
    sum_acc[:, H:] += dot((xw[...].astype(f32) * sent).astype(bf16), pool)
    flow = vecs[2:3, :] * jnp.sum(s0.astype(f32) * dse.astype(f32), axis=0, keepdims=True)
    flow_acc[...] += sum(dot(piece, pool) for piece in parts(flow, 2))


    if half:

        @pl.when(g == pl.num_programs(0) - 1)
        def _():
            close(dc_acc, db_acc, sum_acc, flow_acc, *refs[4:-4])


def close(
    dc, db, sums_far, flow, near, ds_in, sig, b, c, idc, idr, a_log, dround, dlow
):
    rows = lax.broadcasted_iota(jnp.int32, (T, T), 0)
    cols = lax.broadcasted_iota(jnp.int32, (T, T), 1)
    same = (rows >> 7) == (cols >> 7)

    def mask(value):
        return value.astype(f32).astype(bf16)

    def total(where, value, count):
        return sum(dot(mask(where), piece) for piece in parts(value, count))

    row, col = sums_far[:, :H], sums_far[:, H:]
    dla = total(same & (rows > cols), near[:, :H], 3)
    dla += total(same & (rows <= cols), near[:, H : 2 * H], 3)
    dla += total(rows > cols, col, 3) + total(rows <= cols, row, 3) + flow[...]

    def put(span, lanes, value):
        dround[span, lanes] = value.astype(bf16)
        dlow[span, lanes] = (value - value.astype(bf16).astype(f32)).astype(bf16)

    direct = (near[:, 2 * H :] + col) * sig[:, H:]
    put(slice(0, T), slice(2 * N, PROJ), direct - dla * jnp.exp(a_log[...]) * sig[:, :H])
    rows = lax.broadcasted_iota(jnp.int32, (L, L), 0)
    cols = lax.broadcasted_iota(jnp.int32, (L, L), 1)
    for k in range(2):
        span = slice(k * L, (k + 1) * L)
        keep = (idc[span, :] == idr[:, span].astype(f32)) & (rows >= cols)
        ds = ds_in[k]
        kept = jnp.where(keep, ds[:, :L], 0.0)
        to_b = dot(kept, c[span, :], ((0,), (0,)), HIGHEST) + db[span, :]
        to_c = dot(kept, b[span, :], precision=HIGHEST) + dc[span, :]
        if k == 0:
            to_b += ds[:, L:]
        else:
            to_c += ds[:, L:]
        put(span, slice(0, N), to_b)
        put(span, slice(N, 2 * N), to_c)


def post(half, *args):
    def lanes(rows, start=0):
        return block(rows, PL, start)

    def shape(rows, cols, kind=f32):
        return jax.ShapeDtypeStruct((rows, cols), kind)

    accs = ((T, N), (T, N), (T, 2 * H), (1, H))
    ends = (
        (T, 3 * H), (2, L, L + N), (T, 2 * H), (T, N), (T, N), (T, 1), (1, T), (1, H)
    )
    more = [whole(*dims) for dims in accs + ends] + [ANY] * 2 if half else []
    outs = ((T, PROJ, bf16),) * 2 if half else accs
    return pl.pallas_call(
        functools.partial(post_kernel, half) if not half else (
            lambda *refs: post_kernel(half, *refs[:22], *refs[24:])
        ),
        grid=(HALF // PL,),
        out_shape=tuple(shape(*dims) for dims in outs),
        in_specs=[lanes(N)] * 4 + [lanes(T, half * (HALF // PL))] * 2 + [
            lanes(8, half * (HALF // PL)), whole(T, 2 * N), whole(T, 2 * N), whole(8, 1),
        ] + more,
        out_specs=tuple(whole(*dims[:2]) for dims in outs),
        scratch_shapes=[pltpu.VMEM(dims, f32) for dims in accs] if half else [],
        compiler_params=PARAMS,
        cost_estimate=COST,
    )(*args)


def gradw_kernel(pos, ua, ub, da, db, g0, g1, g3, g2a, g2b):
    my_y, my_z = pos[0], pos[1]
    for out, (yo, lo, hi) in zip((g0, g1, g3, g2a, g2b), PLAN):
        for k in range(lo, hi):
            chip = lax.rem(my_y + yo, NY) * NZ + lax.rem(my_z + ORDER[k], NZ)
            at = pl.ds(pl.multiple_of(chip * 64, 64), 64)
            rows = dot(ua[at, :], da[...]) + dot(ub[at, :], db[...])
            out[(k - lo) * 64 : (k - lo + 1) * 64, :] = rows.astype(out.dtype)


def gradw(pos, ua, ub, da, db):
    def shape(rows, kind=bf16):
        return jax.ShapeDtypeStruct((rows, PROJ), kind)

    return pl.pallas_call(
        gradw_kernel,
        out_shape=(shape(512, f32), shape(512), shape(512), shape(256), shape(256)),
        in_specs=[SMEM()] + [VMEM()] * 4,
        out_specs=tuple([VMEM()] * 5),
        compiler_params=SMALL,
        cost_estimate=COST,
    )(pos, ua, ub, da, db)


def gradu_kernel(pos, dhi, dlo, *refs):
    out_u, token, w = refs[-3:]
    token[...] = jnp.zeros_like(token)
    assemble(pos, refs[:10], w)
    last = ((1,), (1,))
    for start in range(0, D, PL):
        rows = w[start : start + PL, :]
        both = dot(dhi[...], rows, last) + dot(dlo[...], rows, last)
        out_u[:, start : start + PL] = both.astype(bf16)


def gradu(pos, dhi, dlo, pieces):
    return pl.pallas_call(
        gradu_kernel,
        out_shape=(jax.ShapeDtypeStruct((T, D), bf16), jax.ShapeDtypeStruct((8, 128), f32)),
        in_specs=[SMEM()] + [VMEM()] * (2 + len(pieces)),
        out_specs=(VMEM(), VMEM()),
        scratch_shapes=[pltpu.VMEM((D, PROJ), bf16)],
        compiler_params=PARAMS,
        cost_estimate=COST,
    )(pos, dhi, dlo, *pieces)


def finish_kernel(half, r1, r2, b1, b2, vecs, bb, cc, flags, x, dy, y, dx, ew2, re2, *refs):
    out_y, out_x, flags_out = refs[-3:]
    flags_out[...] = flags[...]
    ind = head_lanes((pl.program_id(0) + half * (HALF // GL)) * GH, 2, GL, 6)
    s0, dse = arrived(r1, r2, flags, 0), arrived(b1, b2, flags, 1)
    skip = vecs[3:4, :]
    y_off = dot(re2[...], ind) * dot(cc[...], twice(s0))
    out_y[...] = (y[...].astype(f32) + y_off + skip * x[...].astype(f32)).astype(bf16)
    dx_off = dot(ew2[...], ind) * dot(bb[...], twice(dse))
    out_x[...] = (dx[...].astype(f32) + dx_off + skip * dy[...].astype(f32)).astype(bf16)


def finish(half, before, *args):
    shape = jax.ShapeDtypeStruct((T, D), bf16)
    start = half * (HALF // GL)
    wide = block(T, GL, start)
    return pl.pallas_call(
        functools.partial(finish_kernel, half),
        grid=(HALF // GL,),
        out_shape=(shape,) * 2 + (jax.ShapeDtypeStruct((8, 1), f32),),
        in_specs=[block(N)] * 4 + [
            block(8, GL, start), whole(T, 2 * N), whole(T, 2 * N), whole(8, 1),
            wide, wide, wide, wide, whole(T, 2 * H), whole(T, 2 * H),
        ] + [ANY] * len(before),
        out_specs=(wide, wide, whole(8, 1)),
        input_output_aliases={14: 0, 15: 1} if half else {},
        compiler_params=PARAMS,
        cost_estimate=COST,
    )(*args, *before)


def sum_y_kernel(own, up, down, far_a, far_b, token, near, out_up, out_down):
    total = own[...] + up[...].astype(f32) + down[...].astype(f32)
    total += jnp.concatenate([far_a[...], far_b[...]], axis=0).astype(f32)
    near[...] = total[:192]
    out_up[...] = total[192:384].astype(bf16)
    out_down[...] = total[384:].astype(bf16)


def sum_z_kernel(near, up, down, token, here, left, right):
    left[...] = (near[:64] + up[:64].astype(f32)).astype(bf16)
    here[...] = near[64:128] + up[64:128].astype(f32) + down[:64].astype(f32)
    right[...] = (near[128:] + up[128:].astype(f32) + down[64:].astype(f32)).astype(bf16)


def sums(kernel, outs, args, token):
    return pl.pallas_call(
        kernel,
        out_shape=tuple(jax.ShapeDtypeStruct((rows, PROJ), kind) for rows, kind in outs),
        in_specs=[VMEM()] * len(args) + [ANY],
        out_specs=tuple([VMEM()] * len(outs)),
        compiler_params=SMALL,
        cost_estimate=COST,
    )(*args, token)


def body(layer_in, head_in, ids, dy, w_in, a_log, dt_bias, d_skip):
    u, x, dyv = layer_in[0], head_in[0], dy[0]
    dp, seq = lax.axis_index("dp"), lax.axis_index("seq")
    my_y = (dp // (NZ * NC) + 2 * (seq % 2)) % NY
    pos = jnp.stack([my_y, (dp // NC) % NZ, dp % NC, seq]).astype(jnp.int32)
    idr = ids.reshape(1, T)
    a_log, dt_bias, d_skip = (v.reshape(1, H) for v in (a_log, dt_bias, d_skip))

    def odd(k):
        return lambda y, z, c, x: (y + 2 * (x % 2), z + k, c, x)

    left, right = shift(w_in, dz=-1), shift(w_in, dz=1)
    left, u = lax.optimization_barrier((left, u))
    near = jnp.concatenate([left, w_in, right], axis=0)
    high, low, near = fetch(near, odd(3)), fetch(near, odd(-3)), fetch(near, odd(0))

    split = u.reshape(T, NY * NZ, NC, 64)
    mine = lax.dynamic_index_in_dim(split, dp % NC, 2, False)
    other = lax.dynamic_index_in_dim(split, 1 - dp % NC, 2, False)
    ua = mine.transpose(1, 2, 0).reshape(D // 2, T)
    ub = other.transpose(1, 2, 0).reshape(D // 2, T)
    high, low, near, ua, ub, pos, ends = lax.optimization_barrier(
        (high, low, near, ua, ub, pos, ids[0, :: T - 1].astype(bf16))
    )
    row = jnp.concatenate([near, high, low[64:]], axis=0)
    row, ub = lax.optimization_barrier((row, ub))
    ub = shift(ub, dc=1)
    up, down = shift(row, dy=1), shift(row, dy=-1)

    def with_ids(rows):
        return jnp.concatenate([rows, jnp.pad(jnp.broadcast_to(ends, (16, 2)), ((0, 0), (0, PROJ - 2)))], axis=0)

    far_a, far_b = shift(with_ids(row[:256]), dx=1), shift(with_ids(row[256:]), dx=-1)
    own = [row, up, down, far_a, far_b]
    pieces = own + [shift(piece[:512] if i < 3 else piece, dc=1) for i, piece in enumerate(own)]

    (b, c, bb, cc, sig, stept, cumt, cum3, ew2, re2, cross2, vecs, s_a, s_b, g_a,
     g_b, flags, idc) = prep(pos, u, x, dyv, idr, a_log, dt_bias, d_skip, pieces)

    rest = (x, dyv, cumt, stept, cum3, ew2, re2, cross2, b, c, bb, cc, idc, idr, flags)
    r0, b0 = from_seq(s_a, -1), from_seq(g_a, 1)
    first = intra(0, 4, (), *rest)
    one, back = relay(0, s_a, s_b, g_a, g_b, r0, b0, vecs, first[-1])
    r1, b1 = from_seq(one, -1), from_seq(back, 1)
    y_in, dx_in, dyr, xw, sums_in, ds, flags = intra(4, 4, first, *rest)
    one, back = relay(1, s_a, s_b, g_a, g_b, r1, b1, vecs, flags)
    r2, b2 = from_seq(one, -1), from_seq(back, 1)
    shared = (vecs, bb, cc, flags)
    accs = post(0, r0, r1, b0, b1, dyr, xw, *shared)
    local = (x, dyv, y_in, dx_in, ew2, re2)
    *outs, flags = finish(0, (), r0, r1, b0, b1, *shared, *local)
    shared = (vecs, bb, cc, flags)
    dround, dlow = post(
        1, r1, r2, b1, b2, dyr, xw, *shared, *accs, sums_in, ds, sig, b, c,
        idc, idr, a_log, ua, ub,
    )
    dother = shift(dround, dc=1)
    g0, g1, g3, g2a, g2b = gradw(pos, ua, ub, dround, dother)
    parts_y = (
        g0, shift(g1, dy=-1), shift(g3, dy=1), shift(g2a, dx=-1), shift(g2b, dx=1)
    )
    out_u, token = gradu(pos, dround, dlow, pieces)
    near, up, down = sums(sum_y_kernel, ((192, f32), (192, bf16), (128, bf16)), parts_y, token)
    up, down = shift(up, dz=-3), shift(down, dz=3)
    out_y, out_x, token = finish(1, outs, r1, r2, b1, b2, *shared, *local)
    here, left, right = sums(
        sum_z_kernel, ((64, f32), (64, bf16), (64, bf16)), (near, up, down), token
    )
    part = here + shift(right, dz=-1).astype(f32) + shift(left, dz=1).astype(f32)
    grad_w = sum(
        fetch(part, lambda y, z, c, x, k=k: (y + 2 * ((x + k) % 2), z, c, x + k))
        for k in range(NX)
    )
    return out_y[None], out_x[None], out_u[None], grad_w


def solution(mesh):
    return jax.shard_map(
        body,
        mesh=mesh,
        in_specs=(
            P("dp", "seq", None), P("dp", "seq", None), P("dp", "seq"), P("dp", "seq", None),
            P("dp", None), P(), P(), P(),
        ),
        out_specs=(P("dp", "seq", None), P("dp", "seq", None), P("dp", "seq", None), P("dp", None)),
        check_vma=False,
    )
```

```python
import functools

import jax
import jax.numpy as jnp
from jax import lax
from jax.experimental import pallas as pl
from jax.experimental.pallas import tpu as pltpu
from jax.sharding import PartitionSpec as P

bf16, f32 = jnp.bfloat16, jnp.float32
NY, NZ, NC, NX = 4, 8, 2, 4
T, L, D, H, PS, N, PROJ = 256, 128, 4096, 64, 64, 128, 320
GL, GH = 512, 8
PL = 1024
HALF = D // 2
VMEM = functools.partial(pl.BlockSpec, memory_space=pltpu.VMEM)
SMEM = functools.partial(pl.BlockSpec, memory_space=pltpu.SMEM)
PARAMS = pltpu.CompilerParams(vmem_limit_bytes=60 * 1024 * 1024)
SMALL = pltpu.CompilerParams(vmem_limit_bytes=20 * 1024 * 1024)
ANY = pl.BlockSpec(memory_space=pl.ANY)
HIGHEST = lax.Precision.HIGHEST
COST = pl.CostEstimate(flops=1 << 20, bytes_accessed=1 << 16, transcendentals=0)


def fetch(value, source):
    pairs = []
    for y in range(NY):
        for z in range(NZ):
            for c in range(NC):
                for x in range(NX):
                    sy, sz, sc, sx = source(y, z, c, x)
                    at = ((sy % NY * NZ + sz % NZ) * NC + sc % NC) * NX + sx % NX
                    pairs.append((at, ((y * NZ + z) * NC + c) * NX + x))
    return lax.ppermute(value, ("dp", "seq"), pairs)


def shift(value, dy=0, dz=0, dc=0, dx=0):
    return fetch(value, lambda y, z, c, x: (y + dy, z + dz, c + dc, x + dx))


def from_seq(value, offset):
    pairs = [(s + offset, s) for s in range(NX) if 0 <= s + offset < NX]
    return lax.ppermute(value, "seq", pairs)


def dot(a, b, dims=((1,), (0,)), precision=None):
    return lax.dot_general(
        a, b, (dims, ((), ())), preferred_element_type=f32, precision=precision
    )


def parts(value, count):
    out, rest = [], value
    for _ in range(count):
        piece = rest.astype(bf16)
        out.append(piece)
        rest = rest - piece.astype(f32)
    return out


def expand(value, ind, count=2):
    return sum(dot(piece, ind) for piece in parts(value, count))


def head_lanes(first_head, copies, lanes, shift_bits):
    rows = lax.broadcasted_iota(jnp.int32, (copies * H, lanes), 0)
    cols = lax.broadcasted_iota(jnp.int32, (copies * H, lanes), 1)
    return ((rows & (H - 1)) == (cols >> shift_bits) + first_head).astype(f32).astype(bf16)


def lanes_head(first_head, lanes):
    rows = lax.broadcasted_iota(jnp.int32, (lanes, H), 0)
    cols = lax.broadcasted_iota(jnp.int32, (lanes, H), 1)
    return (cols == (rows >> 6) + first_head).astype(f32).astype(bf16)


def put_parts(ref, value, count):
    width = value.shape[1]
    for i, piece in enumerate(parts(value, count)):
        ref[:, i * width : (i + 1) * width] = piece


ORDER = (7, 0, 1, 2, 3, 4, 5, 6)
PLAN = ((0, 0, 8), (1, 0, 8), (3, 0, 8), (2, 0, 4), (2, 4, 8))


def assemble(pos, pieces, w):
    for core in range(2):
        for (yo, lo, hi), piece in zip(PLAN, pieces[5 * core : 5 * core + 5]):
            for k in range(lo, hi):
                owner = (
                    lax.rem(pos[0] + yo, NY) * NZ + lax.rem(pos[1] + ORDER[k], NZ)
                ) * NC + lax.rem(pos[2] + core, NC)
                w[pl.ds(pl.multiple_of(owner * 64, 64), 64), :] = piece[
                    (k - lo) * 64 : (k - lo + 1) * 64, :
                ]


def prep_kernel(pos, u, x_hbm, dy_hbm, idr, a_log, dt_bias, d_skip, *refs):
    pieces, outs = refs[:10], refs[10:]
    (b_out, c_out, bb_out, cc_out, sig_out, stept_out, cumt_out,
     cum3, ew2, re2, cross2, vecs, s_a, s_b, g_a, g_b, flags, idc, w_abs, x, dy, sems) = outs
    copies = [
        pltpu.make_async_copy(source, target, sems.at[i])
        for i, (source, target) in enumerate(((x_hbm, x), (dy_hbm, dy)))
    ]
    for copy in copies:
        copy.start()
    assemble(pos, pieces, w_abs)
    proj = dot(u[...], w_abs[...])
    b, c = proj[:, :N], proj[:, N : 2 * N]
    z = proj[:, 2 * N :] + dt_bias[...]
    small = jnp.exp(-jnp.abs(z))
    step = jnp.maximum(z, 0.0) + jnp.log1p(small)
    sig = jnp.where(z >= 0, 1.0, small) / (1.0 + small)
    sig_out[:, :H] = sig
    tiny = step < 1e-30
    sig_out[:, H:] = jnp.where(tiny, 1.0, sig / jnp.where(tiny, 1.0, step))
    la = -step * jnp.exp(a_log[...])
    rows = lax.broadcasted_iota(jnp.int32, (T, T), 0)
    cols = lax.broadcasted_iota(jnp.int32, (T, T), 1)
    tril = (rows >= cols).astype(f32).astype(bf16)
    cum = sum(dot(tril, piece) for piece in parts(la, 3))
    ids = jnp.broadcast_to(idr[...].astype(f32), (8, T)).T[:, 0:1]
    idc[...] = ids
    id0, idm, ide = ids[0:1], ids[L - 1 : L], ids[T - 1 : T]
    edge = slice(256, 257)
    link = (pieces[4][edge, 1:2].astype(f32) == id0) & (pos[3] > 0)
    linkn = (pieces[3][edge, 0:1].astype(f32) == ide) & (pos[3] < NX - 1)
    link, linkn = jnp.where(link, 1.0, 0.0), jnp.where(linkn, 1.0, 0.0)
    alone = [
        jnp.where(first == final, 1.0, 0.0)
        for first, final in ((id0, ide), *((p[edge, 0:1], p[edge, 1:2]) for p in (pieces[4], pieces[3])))
    ]
    flags[...] = jnp.concatenate([link, linkn] + alone + [link] * 3, axis=0)
    cm, ce = cum[L - 1 : L], cum[T - 1 : T]
    reach = (ids == id0).astype(f32) * jnp.exp(cum)
    end_w = (ids == ide).astype(f32) * jnp.exp(ce - cum) * step
    put_parts(ew2, end_w, 2)
    put_parts(re2, reach, 2)
    a_end = (id0 == ide).astype(f32) * jnp.exp(ce)
    vec = jnp.concatenate(
        [a_end * link, a_end * linkn, a_end, d_skip[...]] * 2, axis=0
    )
    vec_parts = parts(vec, 3)
    put_parts(bb_out, b, 2)
    put_parts(cc_out, c, 2)
    bt = [piece.astype(bf16) for piece in parts(b.T, 2)]
    ct = [piece.astype(bf16) for piece in parts(c.T, 2)]
    for copy in copies:
        copy.wait()
    for g in range(H // GH):
        lanes = slice(g * GL, (g + 1) * GL)
        ind = head_lanes(g * GH, 2, GL, 6)
        xw = (x[:, lanes].astype(f32) * dot(ew2[...], ind)).astype(bf16)
        s_end, g_in = (s_a, g_a) if g < 4 else (s_b, g_b)
        half = slice(g % 4 * GL, (g % 4 + 1) * GL)
        s_end[:, half] = (dot(bt[0], xw) + dot(bt[1], xw)).astype(bf16)
        dyr = (dy[:, lanes].astype(f32) * dot(re2[...], ind)).astype(bf16)
        g_in[:, half] = (dot(ct[0], dyr) + dot(ct[1], dyr)).astype(bf16)
        vecs[:, lanes] = sum(dot(piece, ind[:H]) for piece in vec_parts)
    b_out[...] = b
    c_out[...] = c
    stept_out[...] = step.T
    cumt_out[...] = cum.T
    put_parts(cum3, cum, 3)
    late = (ids[L:] == idm).astype(f32) * jnp.exp(cum[L:] - cm)
    early = (ids[:L] == idm).astype(f32) * jnp.exp(cm - cum[:L])
    put_parts(cross2, jnp.concatenate([early * step[:L], late], axis=0), 2)


def prep(pos, u, x, dy, idr, a_log, dt_bias, d_skip, pieces):
    def shape(rows, cols, kind=f32):
        return jax.ShapeDtypeStruct((rows, cols), kind)

    return pl.pallas_call(
        prep_kernel,
        out_shape=(
            shape(T, N), shape(T, N), shape(T, 2 * N, bf16), shape(T, 2 * N, bf16),
            shape(T, 2 * H), shape(H, T), shape(H, T),
            shape(T, 3 * H, bf16), shape(T, 2 * H, bf16), shape(T, 2 * H, bf16),
            shape(T, 2 * H, bf16), shape(8, D), *(shape(N, HALF, bf16) for _ in range(4)),
            shape(8, 1), shape(T, 1),
        ),
        in_specs=[SMEM(), VMEM()] + [pl.BlockSpec(memory_space=pl.ANY)] * 2
        + [VMEM()] * (4 + len(pieces)),
        out_specs=tuple([VMEM()] * 18),
        scratch_shapes=[
            pltpu.VMEM((D, PROJ), bf16), pltpu.VMEM((T, D), bf16), pltpu.VMEM((T, D), bf16),
            pltpu.SemaphoreType.DMA((2,)),
        ],
        compiler_params=PARAMS,
        cost_estimate=COST,
    )(pos, u, x, dy, idr, a_log, dt_bias, d_skip, *pieces)


def intra_kernel(
    start, x, dy, cumt, stept, cum3, ew2, re2, cross2, b, c, bb, cc, idc, idr, flags, *refs
):
    y_low, dx_low, dyr_out, xw_out, sums_out, ds_out, flags_out, sc, y_out, dx_out = refs[-10:]
    turn = pl.program_id(0)
    g = turn + start
    rows = lax.broadcasted_iota(jnp.int32, (L, L), 0)
    cols = lax.broadcasted_iota(jnp.int32, (L, L), 1)

    @pl.when(turn == 0)
    def _():
        for k in range(2):
            span = slice(k * L, (k + 1) * L)
            scores = dot(c[span, :], b[span, :], ((1,), (1,)), HIGHEST)
            keep = (idc[span, :] == idr[:, span].astype(f32)) & (rows >= cols)
            sc[k] = jnp.where(keep, scores, 0.0)
        flags_out[...] = flags[...]
        for out, before in zip((sums_out, ds_out), refs[:2]):
            out[...] = before[...] if start else jnp.zeros_like(out)

    cum_e = dot(cum3[...], head_lanes(g * GH, 3, GH * L, 7))
    low = lax.broadcasted_iota(jnp.int32, (L, L), 1) < PS
    cumt_g, stept_g = cumt[...], stept[...]
    for k in range(2):
        span = slice(k * L, (k + 1) * L)
        total = jnp.zeros((L, L), f32)
        scores = sc[k]
        for q in range(GH // 2):
            lanes = slice(q * L, (q + 1) * L)
            dyp, xp = dy[span, lanes], x[span, lanes]
            zero = jnp.zeros_like(xp)
            xm = jnp.concatenate([jnp.where(low, xp, zero), jnp.where(low, zero, xp)], axis=0)
            dym = jnp.concatenate([jnp.where(low, dyp, zero), jnp.where(low, zero, dyp)], axis=0)
            grad = dot(dyp, xm, ((1,), (1,)))
            mixing = []
            for half in range(2):
                h = 2 * q + half
                gap = cum_e[span, h * L : (h + 1) * L] - cumt_g[h : h + 1, span]
                e = jnp.exp(jnp.minimum(gap, 0.0)) * stept_g[h : h + 1, span]
                total += e * grad[:, half * L : (half + 1) * L]
                mixing.append((e * scores).astype(bf16))
            y_out[span, lanes] = dot(jnp.concatenate(mixing, axis=1), xm)
            dx_out[span, lanes] = dot(jnp.concatenate(mixing, axis=0), dym, ((0,), (0,)))
        ds_out[k, :, :L] += total
    ind = head_lanes(g * GH, 2, GL, 6)
    pool = lanes_head(g * GH, GL)

    def pooled(value):
        return sum(dot(piece, pool) for piece in parts(value, 2))

    xf, dyf = x[...].astype(f32), dy[...].astype(f32)
    cross = dot(cross2[...], ind)
    xw = (xf[:L] * cross[:L]).astype(bf16)
    dyr = (dyf[L:] * cross[L:]).astype(bf16)
    state = sum(dot(piece, xw) for piece in parts(b[:L, :].T, 2)).astype(bf16)
    back = sum(dot(piece, dyr) for piece in parts(c[L:, :].T, 2)).astype(bf16)
    last = ((1,), (1,))
    ds_out[0, :, L:] += dot(xw, back, last)
    ds_out[1, :, L:] += dot(dyr, state, last)
    read = dot(cc[L:, :], twice(state))
    sent = dot(bb[:L, :], twice(back))
    sums_out[L:, H : 2 * H] += pooled(dyr.astype(f32) * read)
    far = pooled(xw.astype(f32) * sent)
    col = xf * dx_out[...]
    near = pooled(col)
    sums_out[:, :H] += near - pooled(dyf * y_out[...])
    sums_out[:L, :H] += far
    sums_out[:, 2 * H :] += near
    sums_out[:L, 2 * H :] += far
    y_out[L:, :] += cross[L:] * read
    dx_out[:L, :] += cross[:L] * sent
    y_low[...] = y_out[...].astype(bf16)
    dx_low[...] = dx_out[...].astype(bf16)
    xw_out[...] = (xf * dot(ew2[...], ind)).astype(bf16)
    dyr_out[...] = (dyf * dot(re2[...], ind)).astype(bf16)


def whole(*dims):
    return VMEM(dims, lambda i: (0,) * len(dims))


def block(rows, lanes=GL, start=0):
    return VMEM((rows, lanes), lambda i: (0, i + start))


def twice(value):
    return jnp.concatenate([value, value], axis=0)


def intra(start, count, before, x, dy, cumt, stept, cum3, ew2, re2, cross2, b, c, bb, cc, idc,
          idr, flags):
    def shape(*dims, kind=f32):
        return jax.ShapeDtypeStruct(dims, kind)

    heads = VMEM((GH, T), lambda i: (i + start, 0))
    wide = block(T, GL, start)
    return pl.pallas_call(
        functools.partial(intra_kernel, start),
        grid=(count,),
        out_shape=(
            *(shape(T, D, kind=bf16) for _ in range(4)),
            shape(T, 3 * H), shape(2, L, L + N), shape(8, 1),
        ),
        in_specs=[
            wide, wide, heads, heads, whole(T, 3 * H), whole(T, 2 * H),
            whole(T, 2 * H), whole(T, 2 * H), whole(T, N), whole(T, N), whole(T, 2 * N),
            whole(T, 2 * N), whole(T, 1), whole(1, T), whole(8, 1),
        ] + ([whole(T, 3 * H), whole(2, L, L + N)] + [ANY] * 4 if start else []),
        out_specs=(wide, wide, wide, wide, whole(T, 3 * H), whole(2, L, L + N), whole(8, 1)),
        scratch_shapes=[
            pltpu.VMEM((2, L, L), f32), pltpu.VMEM((T, GL), f32), pltpu.VMEM((T, GL), f32)
        ],
        input_output_aliases={17 + i: i for i in range(4)} if start else {},
        compiler_params=PARAMS,
        cost_estimate=COST,
    )(x, dy, cumt, stept, cum3, ew2, re2, cross2, b, c, bb, cc, idc, idr, flags,
      *before[4:6], *before[:4])


def relay_kernel(turn, s_b, g_b, got_s, got_g, vecs, flags, *refs):
    out_s, out_g = refs[-2:]
    s, g = refs[:2] if turn == 0 else (s_b, g_b)
    later = flags[2:3, :] > 0.5
    lanes = slice(turn * HALF, (turn + 1) * HALF)
    for own, last, got, row, out in (
        (s, s_b, got_s, 0, out_s), (g, g_b, got_g, 1, out_g)
    ):
        on = own[...].astype(f32) + vecs[row : row + 1, lanes] * got[...].astype(f32)
        out[...] = jnp.where(later, on, last[...].astype(f32)).astype(bf16)


def relay(turn, *args):
    return pl.pallas_call(
        functools.partial(relay_kernel, turn),
        out_shape=(jax.ShapeDtypeStruct((N, HALF), bf16),) * 2,
        in_specs=[VMEM()] * len(args),
        out_specs=(VMEM(), VMEM()),
        compiler_params=SMALL,
        cost_estimate=COST,
    )(*args)


def arrived(early, late, flags, side):
    one, two = early[...].astype(f32), late[...].astype(f32)
    value = jnp.where(flags[3 + side : 4 + side, :] > 0.5, two, one)
    return (flags[side : side + 1, :] * value).astype(bf16)


def post_kernel(
    half, r1, r2, b1, b2, dyr, xw, vecs, bb, cc, flags, *refs
):
    dc_acc, db_acc, sum_acc, flow_acc = refs[-4:]
    g = pl.program_id(0)

    @pl.when(g == 0)
    def _():
        for acc, before in zip(refs[-4:], refs[:4]):
            acc[...] = before[...] if half else jnp.zeros_like(acc)

    pool = lanes_head((half * (HALF // PL) + g) * (PL // PS), PL)
    s0, dse = arrived(r1, r2, flags, 0), arrived(b1, b2, flags, 1)
    last = ((1,), (1,))
    dc_acc[...] += dot(dyr[...], s0, last)
    db_acc[...] += dot(xw[...], dse, last)
    read, sent = dot(cc[:, :N], s0), dot(bb[:, :N], dse)
    sum_acc[:, :H] += dot((dyr[...].astype(f32) * read).astype(bf16), pool)
    sum_acc[:, H:] += dot((xw[...].astype(f32) * sent).astype(bf16), pool)
    flow = vecs[2:3, :] * jnp.sum(s0.astype(f32) * dse.astype(f32), axis=0, keepdims=True)
    flow_acc[...] += sum(dot(piece, pool) for piece in parts(flow, 2))


    if half:

        @pl.when(g == pl.num_programs(0) - 1)
        def _():
            close(dc_acc, db_acc, sum_acc, flow_acc, *refs[4:-4])


def close(
    dc, db, sums_far, flow, near, ds_in, sig, b, c, idc, idr, a_log, dround, dlow
):
    rows = lax.broadcasted_iota(jnp.int32, (T, T), 0)
    cols = lax.broadcasted_iota(jnp.int32, (T, T), 1)
    same = (rows >> 7) == (cols >> 7)

    def mask(value):
        return value.astype(f32).astype(bf16)

    def total(where, value, count):
        return sum(dot(mask(where), piece) for piece in parts(value, count))

    row, col = sums_far[:, :H], sums_far[:, H:]
    dla = total(same & (rows > cols), near[:, :H], 3)
    dla += total(same & (rows <= cols), near[:, H : 2 * H], 3)
    dla += total(rows > cols, col, 3) + total(rows <= cols, row, 3) + flow[...]

    def put(span, lanes, value):
        dround[span, lanes] = value.astype(bf16)
        dlow[span, lanes] = (value - value.astype(bf16).astype(f32)).astype(bf16)

    direct = (near[:, 2 * H :] + col) * sig[:, H:]
    put(slice(0, T), slice(2 * N, PROJ), direct - dla * jnp.exp(a_log[...]) * sig[:, :H])
    rows = lax.broadcasted_iota(jnp.int32, (L, L), 0)
    cols = lax.broadcasted_iota(jnp.int32, (L, L), 1)
    for k in range(2):
        span = slice(k * L, (k + 1) * L)
        keep = (idc[span, :] == idr[:, span].astype(f32)) & (rows >= cols)
        ds = ds_in[k]
        kept = jnp.where(keep, ds[:, :L], 0.0)
        to_b = dot(kept, c[span, :], ((0,), (0,)), HIGHEST) + db[span, :]
        to_c = dot(kept, b[span, :], precision=HIGHEST) + dc[span, :]
        if k == 0:
            to_b += ds[:, L:]
        else:
            to_c += ds[:, L:]
        put(span, slice(0, N), to_b)
        put(span, slice(N, 2 * N), to_c)


def post(half, *args):
    def lanes(rows, start=0):
        return block(rows, PL, start)

    def shape(rows, cols, kind=f32):
        return jax.ShapeDtypeStruct((rows, cols), kind)

    accs = ((T, N), (T, N), (T, 2 * H), (1, H))
    ends = (
        (T, 3 * H), (2, L, L + N), (T, 2 * H), (T, N), (T, N), (T, 1), (1, T), (1, H)
    )
    more = [whole(*dims) for dims in accs + ends] + [ANY] * 2 if half else []
    outs = ((T, PROJ, bf16),) * 2 if half else accs
    return pl.pallas_call(
        functools.partial(post_kernel, half) if not half else (
            lambda *refs: post_kernel(half, *refs[:22], *refs[24:])
        ),
        grid=(HALF // PL,),
        out_shape=tuple(shape(*dims) for dims in outs),
        in_specs=[lanes(N)] * 4 + [lanes(T, half * (HALF // PL))] * 2 + [
            lanes(8, half * (HALF // PL)), whole(T, 2 * N), whole(T, 2 * N), whole(8, 1),
        ] + more,
        out_specs=tuple(whole(*dims[:2]) for dims in outs),
        scratch_shapes=[pltpu.VMEM(dims, f32) for dims in accs] if half else [],
        compiler_params=PARAMS,
        cost_estimate=COST,
    )(*args)


def gradw_kernel(pos, ua, ub, da, db, g0, g1, g3, g2a, g2b):
    my_y, my_z = pos[0], pos[1]
    for out, (yo, lo, hi) in zip((g0, g1, g3, g2a, g2b), PLAN):
        for k in range(lo, hi):
            chip = lax.rem(my_y + yo, NY) * NZ + lax.rem(my_z + ORDER[k], NZ)
            at = pl.ds(pl.multiple_of(chip * 64, 64), 64)
            rows = dot(ua[at, :], da[...]) + dot(ub[at, :], db[...])
            out[(k - lo) * 64 : (k - lo + 1) * 64, :] = rows.astype(out.dtype)


def gradw(pos, ua, ub, da, db):
    def shape(rows, kind=bf16):
        return jax.ShapeDtypeStruct((rows, PROJ), kind)

    return pl.pallas_call(
        gradw_kernel,
        out_shape=(shape(512, f32), shape(512), shape(512), shape(256), shape(256)),
        in_specs=[SMEM()] + [VMEM()] * 4,
        out_specs=tuple([VMEM()] * 5),
        compiler_params=SMALL,
        cost_estimate=COST,
    )(pos, ua, ub, da, db)


def gradu_kernel(pos, dhi, dlo, *refs):
    out_u, token, w = refs[-3:]
    token[...] = jnp.zeros_like(token)
    assemble(pos, refs[:10], w)
    last = ((1,), (1,))
    for start in range(0, D, PL):
        rows = w[start : start + PL, :]
        both = dot(dhi[...], rows, last) + dot(dlo[...], rows, last)
        out_u[:, start : start + PL] = both.astype(bf16)


def gradu(pos, dhi, dlo, pieces):
    return pl.pallas_call(
        gradu_kernel,
        out_shape=(jax.ShapeDtypeStruct((T, D), bf16), jax.ShapeDtypeStruct((8, 128), f32)),
        in_specs=[SMEM()] + [VMEM()] * (2 + len(pieces)),
        out_specs=(VMEM(), VMEM()),
        scratch_shapes=[pltpu.VMEM((D, PROJ), bf16)],
        compiler_params=PARAMS,
        cost_estimate=COST,
    )(pos, dhi, dlo, *pieces)


def finish_kernel(half, r1, r2, b1, b2, vecs, bb, cc, flags, x, dy, y, dx, ew2, re2, *refs):
    out_y, out_x, flags_out = refs[-3:]
    flags_out[...] = flags[...]
    ind = head_lanes((pl.program_id(0) + half * (HALF // GL)) * GH, 2, GL, 6)
    s0, dse = arrived(r1, r2, flags, 0), arrived(b1, b2, flags, 1)
    skip = vecs[3:4, :]
    y_off = dot(re2[...], ind) * dot(cc[...], twice(s0))
    out_y[...] = (y[...].astype(f32) + y_off + skip * x[...].astype(f32)).astype(bf16)
    dx_off = dot(ew2[...], ind) * dot(bb[...], twice(dse))
    out_x[...] = (dx[...].astype(f32) + dx_off + skip * dy[...].astype(f32)).astype(bf16)


def finish(half, before, *args):
    shape = jax.ShapeDtypeStruct((T, D), bf16)
    start = half * (HALF // GL)
    wide = block(T, GL, start)
    return pl.pallas_call(
        functools.partial(finish_kernel, half),
        grid=(HALF // GL,),
        out_shape=(shape,) * 2 + (jax.ShapeDtypeStruct((8, 1), f32),),
        in_specs=[block(N)] * 4 + [
            block(8, GL, start), whole(T, 2 * N), whole(T, 2 * N), whole(8, 1),
            wide, wide, wide, wide, whole(T, 2 * H), whole(T, 2 * H),
        ] + [ANY] * len(before),
        out_specs=(wide, wide, whole(8, 1)),
        input_output_aliases={14: 0, 15: 1} if half else {},
        compiler_params=PARAMS,
        cost_estimate=COST,
    )(*args, *before)


def sum_y_kernel(own, up, down, far_a, far_b, token, near, out_up, out_down):
    total = own[...] + up[...].astype(f32) + down[...].astype(f32)
    total += jnp.concatenate([far_a[...], far_b[...]], axis=0).astype(f32)
    near[...] = total[:192]
    out_up[...] = total[192:384].astype(bf16)
    out_down[...] = total[384:].astype(bf16)


def sum_z_kernel(near, up, down, token, here, left, right):
    left[...] = (near[:64] + up[:64].astype(f32)).astype(bf16)
    here[...] = near[64:128] + up[64:128].astype(f32) + down[:64].astype(f32)
    right[...] = (near[128:] + up[128:].astype(f32) + down[64:].astype(f32)).astype(bf16)


def sums(kernel, outs, args, token):
    return pl.pallas_call(
        kernel,
        out_shape=tuple(jax.ShapeDtypeStruct((rows, PROJ), kind) for rows, kind in outs),
        in_specs=[VMEM()] * len(args) + [ANY],
        out_specs=tuple([VMEM()] * len(outs)),
        compiler_params=SMALL,
        cost_estimate=COST,
    )(*args, token)


def body(layer_in, head_in, ids, dy, w_in, a_log, dt_bias, d_skip):
    u, x, dyv = layer_in[0], head_in[0], dy[0]
    dp, seq = lax.axis_index("dp"), lax.axis_index("seq")
    my_y = (dp // (NZ * NC) + 2 * (seq % 2)) % NY
    pos = jnp.stack([my_y, (dp // NC) % NZ, dp % NC, seq]).astype(jnp.int32)
    idr = ids.reshape(1, T)
    a_log, dt_bias, d_skip = (v.reshape(1, H) for v in (a_log, dt_bias, d_skip))

    def odd(k):
        return lambda y, z, c, x: (y + 2 * (x % 2), z + k, c, x)

    left, right = shift(w_in, dz=-1), shift(w_in, dz=1)
    left, u = lax.optimization_barrier((left, u))
    near = jnp.concatenate([left, w_in, right], axis=0)
    high, low, near = fetch(near, odd(3)), fetch(near, odd(-3)), fetch(near, odd(0))

    split = u.reshape(T, NY * NZ, NC, 64)
    mine = lax.dynamic_index_in_dim(split, dp % NC, 2, False)
    other = lax.dynamic_index_in_dim(split, 1 - dp % NC, 2, False)
    ua = mine.transpose(1, 2, 0).reshape(D // 2, T)
    ub = other.transpose(1, 2, 0).reshape(D // 2, T)
    high, low, near, ua, ub, pos, ends = lax.optimization_barrier(
        (high, low, near, ua, ub, pos, ids[0, :: T - 1].astype(bf16))
    )
    row = jnp.concatenate([near, high, low[64:]], axis=0)
    row, ub = lax.optimization_barrier((row, ub))
    ub = shift(ub, dc=1)
    up, down = shift(row, dy=1), shift(row, dy=-1)

    def with_ids(rows):
        return jnp.concatenate([rows, jnp.pad(jnp.broadcast_to(ends, (16, 2)), ((0, 0), (0, PROJ - 2)))], axis=0)

    far_a, far_b = shift(with_ids(row[:256]), dx=1), shift(with_ids(row[256:]), dx=-1)
    own = [row, up, down, far_a, far_b]
    pieces = own + [shift(piece[:512] if i < 3 else piece, dc=1) for i, piece in enumerate(own)]

    (b, c, bb, cc, sig, stept, cumt, cum3, ew2, re2, cross2, vecs, s_a, s_b, g_a,
     g_b, flags, idc) = prep(pos, u, x, dyv, idr, a_log, dt_bias, d_skip, pieces)

    rest = (x, dyv, cumt, stept, cum3, ew2, re2, cross2, b, c, bb, cc, idc, idr, flags)
    r0, b0 = from_seq(s_a, -1), from_seq(g_a, 1)
    first = intra(0, 4, (), *rest)
    one, back = relay(0, s_b, g_b, r0, b0, vecs, first[-1], s_a, g_a)
    r1, b1 = from_seq(one, -1), from_seq(back, 1)
    y_in, dx_in, dyr, xw, sums_in, ds, flags = intra(4, 4, first, *rest)
    one, back = relay(1, s_b, g_b, r1, b1, vecs, flags)
    r2, b2 = from_seq(one, -1), from_seq(back, 1)
    shared = (vecs, bb, cc, flags)
    accs = post(0, r0, r1, b0, b1, dyr, xw, *shared)
    local = (x, dyv, y_in, dx_in, ew2, re2)
    *outs, flags = finish(0, (), r0, r1, b0, b1, *shared, *local)
    shared = (vecs, bb, cc, flags)
    dround, dlow = post(
        1, r1, r2, b1, b2, dyr, xw, *shared, *accs, sums_in, ds, sig, b, c,
        idc, idr, a_log, ua, ub,
    )
    dother = shift(dround, dc=1)
    g0, g1, g3, g2a, g2b = gradw(pos, ua, ub, dround, dother)
    parts_y = (
        g0, shift(g1, dy=-1), shift(g3, dy=1), shift(g2a, dx=-1), shift(g2b, dx=1)
    )
    out_u, token = gradu(pos, dround, dlow, pieces)
    near, up, down = sums(sum_y_kernel, ((192, f32), (192, bf16), (128, bf16)), parts_y, token)
    up, down = shift(up, dz=-3), shift(down, dz=3)
    out_y, out_x, token = finish(1, outs, r1, r2, b1, b2, *shared, *local)
    here, left, right = sums(
        sum_z_kernel, ((64, f32), (64, bf16), (64, bf16)), (near, up, down), token
    )
    part = here + shift(right, dz=-1).astype(f32) + shift(left, dz=1).astype(f32)
    part = part.astype(bf16)
    grad_w = sum(
        fetch(part, lambda y, z, c, x, k=k: (y + 2 * ((x + k) % 2), z, c, x + k)).astype(f32)
        for k in range(NX)
    )
    return out_y[None], out_x[None], out_u[None], grad_w


def solution(mesh):
    return jax.shard_map(
        body,
        mesh=mesh,
        in_specs=(
            P("dp", "seq", None), P("dp", "seq", None), P("dp", "seq"), P("dp", "seq", None),
            P("dp", None), P(), P(), P(),
        ),
        out_specs=(P("dp", "seq", None), P("dp", "seq", None), P("dp", "seq", None), P("dp", None)),
        check_vma=False,
    )
```

```python
import functools

import jax
import jax.numpy as jnp
from jax import lax
from jax.experimental import pallas as pl
from jax.experimental.pallas import tpu as pltpu
from jax.sharding import PartitionSpec as P

bf16, f32 = jnp.bfloat16, jnp.float32
NY, NZ, NC, NX = 4, 8, 2, 4
T, L, D, H, PS, N, PROJ = 256, 128, 4096, 64, 64, 128, 320
GL, GH = 512, 8
PL = 1024
HALF = D // 2
VMEM = functools.partial(pl.BlockSpec, memory_space=pltpu.VMEM)
SMEM = functools.partial(pl.BlockSpec, memory_space=pltpu.SMEM)
PARAMS = pltpu.CompilerParams(vmem_limit_bytes=60 * 1024 * 1024)
SMALL = pltpu.CompilerParams(vmem_limit_bytes=20 * 1024 * 1024)
ANY = pl.BlockSpec(memory_space=pl.ANY)
HIGHEST = lax.Precision.HIGHEST
COST = pl.CostEstimate(flops=1 << 20, bytes_accessed=1 << 16, transcendentals=0)


def fetch(value, source):
    pairs = []
    for y in range(NY):
        for z in range(NZ):
            for c in range(NC):
                for x in range(NX):
                    sy, sz, sc, sx = source(y, z, c, x)
                    at = ((sy % NY * NZ + sz % NZ) * NC + sc % NC) * NX + sx % NX
                    pairs.append((at, ((y * NZ + z) * NC + c) * NX + x))
    return lax.ppermute(value, ("dp", "seq"), pairs)


def shift(value, dy=0, dz=0, dc=0, dx=0):
    return fetch(value, lambda y, z, c, x: (y + dy, z + dz, c + dc, x + dx))


def from_seq(value, offset):
    pairs = [(s + offset, s) for s in range(NX) if 0 <= s + offset < NX]
    return lax.ppermute(value, "seq", pairs)


def dot(a, b, dims=((1,), (0,)), precision=None):
    return lax.dot_general(
        a, b, (dims, ((), ())), preferred_element_type=f32, precision=precision
    )


def parts(value, count):
    out, rest = [], value
    for _ in range(count):
        piece = rest.astype(bf16)
        out.append(piece)
        rest = rest - piece.astype(f32)
    return out


def expand(value, ind, count=2):
    return sum(dot(piece, ind) for piece in parts(value, count))


def head_lanes(first_head, copies, lanes, shift_bits):
    rows = lax.broadcasted_iota(jnp.int32, (copies * H, lanes), 0)
    cols = lax.broadcasted_iota(jnp.int32, (copies * H, lanes), 1)
    return ((rows & (H - 1)) == (cols >> shift_bits) + first_head).astype(f32).astype(bf16)


def lanes_head(first_head, lanes):
    rows = lax.broadcasted_iota(jnp.int32, (lanes, H), 0)
    cols = lax.broadcasted_iota(jnp.int32, (lanes, H), 1)
    return (cols == (rows >> 6) + first_head).astype(f32).astype(bf16)


def put_parts(ref, value, count):
    width = value.shape[1]
    for i, piece in enumerate(parts(value, count)):
        ref[:, i * width : (i + 1) * width] = piece


ORDER = (7, 0, 1, 2, 3, 4, 5, 6)
PLAN = ((0, 0, 8), (1, 0, 8), (3, 0, 8), (2, 0, 4), (2, 4, 8))


def assemble(pos, pieces, w):
    for core in range(2):
        for (yo, lo, hi), piece in zip(PLAN, pieces[5 * core : 5 * core + 5]):
            for k in range(lo, hi):
                owner = (
                    lax.rem(pos[0] + yo, NY) * NZ + lax.rem(pos[1] + ORDER[k], NZ)
                ) * NC + lax.rem(pos[2] + core, NC)
                w[pl.ds(pl.multiple_of(owner * 64, 64), 64), :] = piece[
                    (k - lo) * 64 : (k - lo + 1) * 64, :
                ]


def prep_kernel(pos, u, x_hbm, dy_hbm, idr, a_log, dt_bias, d_skip, *refs):
    pieces, outs = refs[:10], refs[10:]
    (b_out, c_out, bb_out, cc_out, sig_out, stept_out, cumt_out,
     cum3, ew2, re2, cross2, vecs, s_a, s_b, g_a, g_b, flags, idc, w_abs, x, dy, sems) = outs
    copies = [
        pltpu.make_async_copy(source, target, sems.at[i])
        for i, (source, target) in enumerate(((x_hbm, x), (dy_hbm, dy)))
    ]
    for copy in copies:
        copy.start()
    assemble(pos, pieces, w_abs)
    proj = dot(u[...], w_abs[...])
    b, c = proj[:, :N], proj[:, N : 2 * N]
    z = proj[:, 2 * N :] + dt_bias[...]
    small = jnp.exp(-jnp.abs(z))
    step = jnp.maximum(z, 0.0) + jnp.log1p(small)
    sig = jnp.where(z >= 0, 1.0, small) / (1.0 + small)
    sig_out[:, :H] = sig
    tiny = step < 1e-30
    sig_out[:, H:] = jnp.where(tiny, 1.0, sig / jnp.where(tiny, 1.0, step))
    la = -step * jnp.exp(a_log[...])
    rows = lax.broadcasted_iota(jnp.int32, (T, T), 0)
    cols = lax.broadcasted_iota(jnp.int32, (T, T), 1)
    tril = (rows >= cols).astype(f32).astype(bf16)
    cum = sum(dot(tril, piece) for piece in parts(la, 3))
    ids = jnp.broadcast_to(idr[...].astype(f32), (8, T)).T[:, 0:1]
    idc[...] = ids
    id0, idm, ide = ids[0:1], ids[L - 1 : L], ids[T - 1 : T]
    edge = slice(256, 257)
    link = (pieces[4][edge, 1:2].astype(f32) == id0) & (pos[3] > 0)
    linkn = (pieces[3][edge, 0:1].astype(f32) == ide) & (pos[3] < NX - 1)
    link, linkn = jnp.where(link, 1.0, 0.0), jnp.where(linkn, 1.0, 0.0)
    alone = [
        jnp.where(first == final, 1.0, 0.0)
        for first, final in ((id0, ide), *((p[edge, 0:1], p[edge, 1:2]) for p in (pieces[4], pieces[3])))
    ]
    flags[...] = jnp.concatenate([link, linkn] + alone + [link] * 3, axis=0)
    cm, ce = cum[L - 1 : L], cum[T - 1 : T]
    reach = (ids == id0).astype(f32) * jnp.exp(cum)
    end_w = (ids == ide).astype(f32) * jnp.exp(ce - cum) * step
    put_parts(ew2, end_w, 2)
    put_parts(re2, reach, 2)
    a_end = (id0 == ide).astype(f32) * jnp.exp(ce)
    vec = jnp.concatenate(
        [a_end * link, a_end * linkn, a_end, d_skip[...]] * 2, axis=0
    )
    vec_parts = parts(vec, 3)
    put_parts(bb_out, b, 2)
    put_parts(cc_out, c, 2)
    bt = [piece.astype(bf16) for piece in parts(b.T, 2)]
    ct = [piece.astype(bf16) for piece in parts(c.T, 2)]
    for copy in copies:
        copy.wait()
    for g in range(H // GH):
        lanes = slice(g * GL, (g + 1) * GL)
        ind = head_lanes(g * GH, 2, GL, 6)
        xw = (x[:, lanes].astype(f32) * dot(ew2[...], ind)).astype(bf16)
        s_end, g_in = (s_a, g_a) if g < 4 else (s_b, g_b)
        half = slice(g % 4 * GL, (g % 4 + 1) * GL)
        s_end[:, half] = (dot(bt[0], xw) + dot(bt[1], xw)).astype(bf16)
        dyr = (dy[:, lanes].astype(f32) * dot(re2[...], ind)).astype(bf16)
        g_in[:, half] = (dot(ct[0], dyr) + dot(ct[1], dyr)).astype(bf16)
        vecs[:, lanes] = sum(dot(piece, ind[:H]) for piece in vec_parts)
    b_out[...] = b
    c_out[...] = c
    stept_out[...] = step.T
    cumt_out[...] = cum.T
    put_parts(cum3, cum, 3)
    late = (ids[L:] == idm).astype(f32) * jnp.exp(cum[L:] - cm)
    early = (ids[:L] == idm).astype(f32) * jnp.exp(cm - cum[:L])
    put_parts(cross2, jnp.concatenate([early * step[:L], late], axis=0), 2)


def prep(pos, u, x, dy, idr, a_log, dt_bias, d_skip, pieces):
    def shape(rows, cols, kind=f32):
        return jax.ShapeDtypeStruct((rows, cols), kind)

    return pl.pallas_call(
        prep_kernel,
        out_shape=(
            shape(T, N), shape(T, N), shape(T, 2 * N, bf16), shape(T, 2 * N, bf16),
            shape(T, 2 * H), shape(H, T), shape(H, T),
            shape(T, 3 * H, bf16), shape(T, 2 * H, bf16), shape(T, 2 * H, bf16),
            shape(T, 2 * H, bf16), shape(8, D), *(shape(N, HALF, bf16) for _ in range(4)),
            shape(8, 1), shape(T, 1),
        ),
        in_specs=[SMEM(), VMEM()] + [pl.BlockSpec(memory_space=pl.ANY)] * 2
        + [VMEM()] * (4 + len(pieces)),
        out_specs=tuple([VMEM()] * 18),
        scratch_shapes=[
            pltpu.VMEM((D, PROJ), bf16), pltpu.VMEM((T, D), bf16), pltpu.VMEM((T, D), bf16),
            pltpu.SemaphoreType.DMA((2,)),
        ],
        compiler_params=PARAMS,
        cost_estimate=COST,
    )(pos, u, x, dy, idr, a_log, dt_bias, d_skip, *pieces)


def intra_kernel(
    start, x, dy, cumt, stept, cum3, ew2, re2, cross2, b, c, bb, cc, idc, idr, flags, *refs
):
    y_low, dx_low, dyr_out, xw_out, sums_out, ds_out, flags_out, sc, y_out, dx_out = refs[-10:]
    turn = pl.program_id(0)
    g = turn + start
    rows = lax.broadcasted_iota(jnp.int32, (L, L), 0)
    cols = lax.broadcasted_iota(jnp.int32, (L, L), 1)

    @pl.when(turn == 0)
    def _():
        for k in range(2):
            span = slice(k * L, (k + 1) * L)
            scores = dot(c[span, :], b[span, :], ((1,), (1,)), HIGHEST)
            keep = (idc[span, :] == idr[:, span].astype(f32)) & (rows >= cols)
            sc[k] = jnp.where(keep, scores, 0.0)
        flags_out[...] = flags[...]
        for out, before in zip((sums_out, ds_out), refs[:2]):
            out[...] = before[...] if start else jnp.zeros_like(out)

    cum_e = dot(cum3[...], head_lanes(g * GH, 3, GH * L, 7))
    low = lax.broadcasted_iota(jnp.int32, (L, L), 1) < PS
    cumt_g, stept_g = cumt[...], stept[...]
    for k in range(2):
        span = slice(k * L, (k + 1) * L)
        total = jnp.zeros((L, L), f32)
        scores = sc[k]
        for q in range(GH // 2):
            lanes = slice(q * L, (q + 1) * L)
            dyp, xp = dy[span, lanes], x[span, lanes]
            zero = jnp.zeros_like(xp)
            xm = jnp.concatenate([jnp.where(low, xp, zero), jnp.where(low, zero, xp)], axis=0)
            dym = jnp.concatenate([jnp.where(low, dyp, zero), jnp.where(low, zero, dyp)], axis=0)
            grad = dot(dyp, xm, ((1,), (1,)))
            mixing = []
            for half in range(2):
                h = 2 * q + half
                gap = cum_e[span, h * L : (h + 1) * L] - cumt_g[h : h + 1, span]
                e = jnp.exp(jnp.minimum(gap, 0.0)) * stept_g[h : h + 1, span]
                total += e * grad[:, half * L : (half + 1) * L]
                mixing.append((e * scores).astype(bf16))
            y_out[span, lanes] = dot(jnp.concatenate(mixing, axis=1), xm)
            dx_out[span, lanes] = dot(jnp.concatenate(mixing, axis=0), dym, ((0,), (0,)))
        ds_out[k, :, :L] += total
    ind = head_lanes(g * GH, 2, GL, 6)
    pool = lanes_head(g * GH, GL)

    def pooled(value):
        return sum(dot(piece, pool) for piece in parts(value, 2))

    xf, dyf = x[...].astype(f32), dy[...].astype(f32)
    cross = dot(cross2[...], ind)
    xw = (xf[:L] * cross[:L]).astype(bf16)
    dyr = (dyf[L:] * cross[L:]).astype(bf16)
    state = sum(dot(piece, xw) for piece in parts(b[:L, :].T, 2)).astype(bf16)
    back = sum(dot(piece, dyr) for piece in parts(c[L:, :].T, 2)).astype(bf16)
    last = ((1,), (1,))
    ds_out[0, :, L:] += dot(xw, back, last)
    ds_out[1, :, L:] += dot(dyr, state, last)
    read = dot(cc[L:, :], twice(state))
    sent = dot(bb[:L, :], twice(back))
    sums_out[L:, H : 2 * H] += pooled(dyr.astype(f32) * read)
    far = pooled(xw.astype(f32) * sent)
    col = xf * dx_out[...]
    near = pooled(col)
    sums_out[:, :H] += near - pooled(dyf * y_out[...])
    sums_out[:L, :H] += far
    sums_out[:, 2 * H :] += near
    sums_out[:L, 2 * H :] += far
    y_out[L:, :] += cross[L:] * read
    dx_out[:L, :] += cross[:L] * sent
    y_low[...] = y_out[...].astype(bf16)
    dx_low[...] = dx_out[...].astype(bf16)
    xw_out[...] = (xf * dot(ew2[...], ind)).astype(bf16)
    dyr_out[...] = (dyf * dot(re2[...], ind)).astype(bf16)


def whole(*dims):
    return VMEM(dims, lambda i: (0,) * len(dims))


def block(rows, lanes=GL, start=0):
    return VMEM((rows, lanes), lambda i: (0, i + start))


def twice(value):
    return jnp.concatenate([value, value], axis=0)


def intra(start, count, before, x, dy, cumt, stept, cum3, ew2, re2, cross2, b, c, bb, cc, idc,
          idr, flags):
    def shape(*dims, kind=f32):
        return jax.ShapeDtypeStruct(dims, kind)

    heads = VMEM((GH, T), lambda i: (i + start, 0))
    wide = block(T, GL, start)
    return pl.pallas_call(
        functools.partial(intra_kernel, start),
        grid=(count,),
        out_shape=(
            *(shape(T, D, kind=bf16) for _ in range(4)),
            shape(T, 3 * H), shape(2, L, L + N), shape(8, 1),
        ),
        in_specs=[
            wide, wide, heads, heads, whole(T, 3 * H), whole(T, 2 * H),
            whole(T, 2 * H), whole(T, 2 * H), whole(T, N), whole(T, N), whole(T, 2 * N),
            whole(T, 2 * N), whole(T, 1), whole(1, T), whole(8, 1),
        ] + ([whole(T, 3 * H), whole(2, L, L + N)] + [ANY] * 4 if start else []),
        out_specs=(wide, wide, wide, wide, whole(T, 3 * H), whole(2, L, L + N), whole(8, 1)),
        scratch_shapes=[
            pltpu.VMEM((2, L, L), f32), pltpu.VMEM((T, GL), f32), pltpu.VMEM((T, GL), f32)
        ],
        input_output_aliases={17 + i: i for i in range(4)} if start else {},
        compiler_params=PARAMS,
        cost_estimate=COST,
    )(x, dy, cumt, stept, cum3, ew2, re2, cross2, b, c, bb, cc, idc, idr, flags,
      *before[4:6], *before[:4])


def relay_kernel(turn, s_b, g_b, got_s, got_g, vecs, flags, *refs):
    out_s, out_g = refs[-2:]
    s, g = refs[:2] if turn == 0 else (s_b, g_b)
    later = flags[2:3, :] > 0.5
    lanes = slice(turn * HALF, (turn + 1) * HALF)
    for own, last, got, row, out in (
        (s, s_b, got_s, 0, out_s), (g, g_b, got_g, 1, out_g)
    ):
        on = own[...].astype(f32) + vecs[row : row + 1, lanes] * got[...].astype(f32)
        out[...] = jnp.where(later, on, last[...].astype(f32)).astype(bf16)


def relay(turn, *args):
    return pl.pallas_call(
        functools.partial(relay_kernel, turn),
        out_shape=(jax.ShapeDtypeStruct((N, HALF), bf16),) * 2,
        in_specs=[VMEM()] * len(args),
        out_specs=(VMEM(), VMEM()),
        compiler_params=SMALL,
        cost_estimate=COST,
    )(*args)


def arrived(early, late, flags, side):
    one, two = early[...].astype(f32), late[...].astype(f32)
    value = jnp.where(flags[3 + side : 4 + side, :] > 0.5, two, one)
    return (flags[side : side + 1, :] * value).astype(bf16)


def post_kernel(
    half, r1, r2, b1, b2, dyr, xw, vecs, bb, cc, flags, *refs
):
    accs = refs[-4:] if half else refs[8:12]
    dc_acc, db_acc, sum_acc, flow_acc = accs
    g = pl.program_id(0)

    @pl.when(g == 0)
    def _():
        for acc, before in zip(accs, refs[:4]):
            acc[...] = before[...] if half else jnp.zeros_like(acc)

    pool = lanes_head((half * (HALF // PL) + g) * (PL // PS), PL)
    s0, dse = arrived(r1, r2, flags, 0), arrived(b1, b2, flags, 1)
    last = ((1,), (1,))
    dc_acc[...] += dot(dyr[...], s0, last)
    db_acc[...] += dot(xw[...], dse, last)
    read, sent = dot(cc[:, :N], s0), dot(bb[:, :N], dse)
    sum_acc[:, :H] += dot((dyr[...].astype(f32) * read).astype(bf16), pool)
    sum_acc[:, H:] += dot((xw[...].astype(f32) * sent).astype(bf16), pool)
    flow = vecs[2:3, :] * jnp.sum(s0.astype(f32) * dse.astype(f32), axis=0, keepdims=True)
    flow_acc[...] += sum(dot(piece, pool) for piece in parts(flow, 2))


    @pl.when(g == pl.num_programs(0) - 1)
    def _():
        if half:
            close(*accs, *refs[4:9])
        else:
            within(*refs[:8], refs[12])


def mask_total(where, value, count):
    where = where.astype(f32).astype(bf16)
    return sum(dot(where, piece) for piece in parts(value, count))


def within(near, ds_in, sig, b, c, idc, idr, a_log, local):
    rows = lax.broadcasted_iota(jnp.int32, (T, T), 0)
    cols = lax.broadcasted_iota(jnp.int32, (T, T), 1)
    same = (rows >> 7) == (cols >> 7)
    dla = mask_total(same & (rows > cols), near[:, :H], 3)
    dla += mask_total(same & (rows <= cols), near[:, H : 2 * H], 3)
    direct = near[:, 2 * H :] * sig[:, H:]
    local[:, 2 * N :] = direct - dla * jnp.exp(a_log[...]) * sig[:, :H]
    rows = lax.broadcasted_iota(jnp.int32, (L, L), 0)
    cols = lax.broadcasted_iota(jnp.int32, (L, L), 1)
    for k in range(2):
        span = slice(k * L, (k + 1) * L)
        keep = (idc[span, :] == idr[:, span].astype(f32)) & (rows >= cols)
        ds = ds_in[k]
        kept = jnp.where(keep, ds[:, :L], 0.0)
        to_b = dot(kept, c[span, :], ((0,), (0,)), HIGHEST)
        to_c = dot(kept, b[span, :], precision=HIGHEST)
        if k == 0:
            to_b += ds[:, L:]
        else:
            to_c += ds[:, L:]
        local[span, :N] = to_b
        local[span, N : 2 * N] = to_c


def close(dc, db, sums_far, flow, local, sig, a_log, dround, dlow):
    rows = lax.broadcasted_iota(jnp.int32, (T, T), 0)
    cols = lax.broadcasted_iota(jnp.int32, (T, T), 1)
    row, col = sums_far[:, :H], sums_far[:, H:]
    dla = mask_total(rows > cols, col, 3) + mask_total(rows <= cols, row, 3) + flow[...]
    step = col * sig[:, H:] - dla * jnp.exp(a_log[...]) * sig[:, :H]
    for lanes, far in (
        (slice(0, N), db[...]), (slice(N, 2 * N), dc[...]), (slice(2 * N, PROJ), step)
    ):
        value = local[:, lanes] + far
        dround[:, lanes] = value.astype(bf16)
        dlow[:, lanes] = (value - value.astype(bf16).astype(f32)).astype(bf16)


def post(half, *args):
    def lanes(rows, start=0):
        return block(rows, PL, start)

    def shape(rows, cols, kind=f32):
        return jax.ShapeDtypeStruct((rows, cols), kind)

    accs = ((T, N), (T, N), (T, 2 * H), (1, H))
    ends = (
        (T, 3 * H), (2, L, L + N), (T, 2 * H), (T, N), (T, N), (T, 1), (1, T), (1, H)
    )
    late = accs + ((T, PROJ), (T, 2 * H), (1, H))
    more = [whole(*dims) for dims in (late if half else ends)] + [ANY] * (2 * half)
    outs = ((T, PROJ, bf16),) * 2 if half else accs + ((T, PROJ),)
    return pl.pallas_call(
        functools.partial(post_kernel, half) if not half else (
            lambda *refs: post_kernel(half, *refs[:17], *refs[19:])
        ),
        grid=(HALF // PL,),
        out_shape=tuple(shape(*dims) for dims in outs),
        in_specs=[lanes(N)] * 4 + [lanes(T, half * (HALF // PL))] * 2 + [
            lanes(8, half * (HALF // PL)), whole(T, 2 * N), whole(T, 2 * N), whole(8, 1),
        ] + more,
        out_specs=tuple(whole(*dims[:2]) for dims in outs),
        scratch_shapes=[pltpu.VMEM(dims, f32) for dims in accs] if half else [],
        compiler_params=PARAMS,
        cost_estimate=COST,
    )(*args)


def gradw_kernel(pos, ua, ub, da, db, g0, g1, g3, g2a, g2b):
    my_y, my_z = pos[0], pos[1]
    for out, (yo, lo, hi) in zip((g0, g1, g3, g2a, g2b), PLAN):
        for k in range(lo, hi):
            chip = lax.rem(my_y + yo, NY) * NZ + lax.rem(my_z + ORDER[k], NZ)
            at = pl.ds(pl.multiple_of(chip * 64, 64), 64)
            rows = dot(ua[at, :], da[...]) + dot(ub[at, :], db[...])
            out[(k - lo) * 64 : (k - lo + 1) * 64, :] = rows.astype(out.dtype)


def gradw(pos, ua, ub, da, db):
    def shape(rows, kind=bf16):
        return jax.ShapeDtypeStruct((rows, PROJ), kind)

    return pl.pallas_call(
        gradw_kernel,
        out_shape=(shape(512, f32), shape(512), shape(512), shape(256), shape(256)),
        in_specs=[SMEM()] + [VMEM()] * 4,
        out_specs=tuple([VMEM()] * 5),
        compiler_params=SMALL,
        cost_estimate=COST,
    )(pos, ua, ub, da, db)


def gradu_kernel(pos, dhi, dlo, *refs):
    out_u, token, w = refs[-3:]
    token[...] = jnp.zeros_like(token)
    assemble(pos, refs[:10], w)
    last = ((1,), (1,))
    for start in range(0, D, PL):
        rows = w[start : start + PL, :]
        both = dot(dhi[...], rows, last) + dot(dlo[...], rows, last)
        out_u[:, start : start + PL] = both.astype(bf16)


def gradu(pos, dhi, dlo, pieces):
    return pl.pallas_call(
        gradu_kernel,
        out_shape=(jax.ShapeDtypeStruct((T, D), bf16), jax.ShapeDtypeStruct((8, 128), f32)),
        in_specs=[SMEM()] + [VMEM()] * (2 + len(pieces)),
        out_specs=(VMEM(), VMEM()),
        scratch_shapes=[pltpu.VMEM((D, PROJ), bf16)],
        compiler_params=PARAMS,
        cost_estimate=COST,
    )(pos, dhi, dlo, *pieces)


def finish_kernel(half, r1, r2, b1, b2, vecs, bb, cc, flags, x, dy, y, dx, ew2, re2, *refs):
    out_y, out_x, flags_out = refs[-3:]
    flags_out[...] = flags[...]
    ind = head_lanes((pl.program_id(0) + half * (HALF // GL)) * GH, 2, GL, 6)
    s0, dse = arrived(r1, r2, flags, 0), arrived(b1, b2, flags, 1)
    skip = vecs[3:4, :]
    y_off = dot(re2[...], ind) * dot(cc[...], twice(s0))
    out_y[...] = (y[...].astype(f32) + y_off + skip * x[...].astype(f32)).astype(bf16)
    dx_off = dot(ew2[...], ind) * dot(bb[...], twice(dse))
    out_x[...] = (dx[...].astype(f32) + dx_off + skip * dy[...].astype(f32)).astype(bf16)


def finish(half, before, *args):
    shape = jax.ShapeDtypeStruct((T, D), bf16)
    start = half * (HALF // GL)
    wide = block(T, GL, start)
    return pl.pallas_call(
        functools.partial(finish_kernel, half),
        grid=(HALF // GL,),
        out_shape=(shape,) * 2 + (jax.ShapeDtypeStruct((8, 1), f32),),
        in_specs=[block(N)] * 4 + [
            block(8, GL, start), whole(T, 2 * N), whole(T, 2 * N), whole(8, 1),
            wide, wide, wide, wide, whole(T, 2 * H), whole(T, 2 * H),
        ] + [ANY] * len(before),
        out_specs=(wide, wide, whole(8, 1)),
        input_output_aliases={14: 0, 15: 1} if half else {},
        compiler_params=PARAMS,
        cost_estimate=COST,
    )(*args, *before)


def sum_y_kernel(own, up, down, far_a, far_b, token, near, out_up, out_down):
    total = own[...] + up[...].astype(f32) + down[...].astype(f32)
    total += jnp.concatenate([far_a[...], far_b[...]], axis=0).astype(f32)
    near[...] = total[:192]
    out_up[...] = total[192:384].astype(bf16)
    out_down[...] = total[384:].astype(bf16)


def sum_z_kernel(near, up, down, token, here, left, right):
    left[...] = (near[:64] + up[:64].astype(f32)).astype(bf16)
    here[...] = near[64:128] + up[64:128].astype(f32) + down[:64].astype(f32)
    right[...] = (near[128:] + up[128:].astype(f32) + down[64:].astype(f32)).astype(bf16)


def sums(kernel, outs, args, token):
    return pl.pallas_call(
        kernel,
        out_shape=tuple(jax.ShapeDtypeStruct((rows, PROJ), kind) for rows, kind in outs),
        in_specs=[VMEM()] * len(args) + [ANY],
        out_specs=tuple([VMEM()] * len(outs)),
        compiler_params=SMALL,
        cost_estimate=COST,
    )(*args, token)


def body(layer_in, head_in, ids, dy, w_in, a_log, dt_bias, d_skip):
    u, x, dyv = layer_in[0], head_in[0], dy[0]
    dp, seq = lax.axis_index("dp"), lax.axis_index("seq")
    my_y = (dp // (NZ * NC) + 2 * (seq % 2)) % NY
    pos = jnp.stack([my_y, (dp // NC) % NZ, dp % NC, seq]).astype(jnp.int32)
    idr = ids.reshape(1, T)
    a_log, dt_bias, d_skip = (v.reshape(1, H) for v in (a_log, dt_bias, d_skip))

    def odd(k):
        return lambda y, z, c, x: (y + 2 * (x % 2), z + k, c, x)

    left, right = shift(w_in, dz=-1), shift(w_in, dz=1)
    left, u = lax.optimization_barrier((left, u))
    near = jnp.concatenate([left, w_in, right], axis=0)
    high, low, near = fetch(near, odd(3)), fetch(near, odd(-3)), fetch(near, odd(0))

    split = u.reshape(T, NY * NZ, NC, 64)
    mine = lax.dynamic_index_in_dim(split, dp % NC, 2, False)
    other = lax.dynamic_index_in_dim(split, 1 - dp % NC, 2, False)
    ua = mine.transpose(1, 2, 0).reshape(D // 2, T)
    ub = other.transpose(1, 2, 0).reshape(D // 2, T)
    high, low, near, ua, ub, pos, ends = lax.optimization_barrier(
        (high, low, near, ua, ub, pos, ids[0, :: T - 1].astype(bf16))
    )
    row = jnp.concatenate([near, high, low[64:]], axis=0)
    row, ub = lax.optimization_barrier((row, ub))
    ub = shift(ub, dc=1)
    up, down = shift(row, dy=1), shift(row, dy=-1)

    def with_ids(rows):
        return jnp.concatenate([rows, jnp.pad(jnp.broadcast_to(ends, (16, 2)), ((0, 0), (0, PROJ - 2)))], axis=0)

    far_a, far_b = shift(with_ids(row[:256]), dx=1), shift(with_ids(row[256:]), dx=-1)
    own = [row, up, down, far_a, far_b]
    pieces = own + [shift(piece[:512] if i < 3 else piece, dc=1) for i, piece in enumerate(own)]

    (b, c, bb, cc, sig, stept, cumt, cum3, ew2, re2, cross2, vecs, s_a, s_b, g_a,
     g_b, flags, idc) = prep(pos, u, x, dyv, idr, a_log, dt_bias, d_skip, pieces)

    rest = (x, dyv, cumt, stept, cum3, ew2, re2, cross2, b, c, bb, cc, idc, idr, flags)
    r0, b0 = from_seq(s_a, -1), from_seq(g_a, 1)
    first = intra(0, 4, (), *rest)
    one, back = relay(0, s_b, g_b, r0, b0, vecs, first[-1], s_a, g_a)
    r1, b1 = from_seq(one, -1), from_seq(back, 1)
    y_in, dx_in, dyr, xw, sums_in, ds, flags = intra(4, 4, first, *rest)
    one, back = relay(1, s_b, g_b, r1, b1, vecs, flags)
    r2, b2 = from_seq(one, -1), from_seq(back, 1)
    shared = (vecs, bb, cc, flags)
    accs = post(
        0, r0, r1, b0, b1, dyr, xw, *shared, sums_in, ds, sig, b, c, idc, idr, a_log
    )
    local = (x, dyv, y_in, dx_in, ew2, re2)
    *outs, flags = finish(0, (), r0, r1, b0, b1, *shared, *local)
    shared = (vecs, bb, cc, flags)
    dround, dlow = post(
        1, r1, r2, b1, b2, dyr, xw, *shared, *accs, sig, a_log, ua, ub,
    )
    dother = shift(dround, dc=1)
    g0, g1, g3, g2a, g2b = gradw(pos, ua, ub, dround, dother)
    parts_y = (
        g0, shift(g1, dy=-1), shift(g3, dy=1), shift(g2a, dx=-1), shift(g2b, dx=1)
    )
    out_u, token = gradu(pos, dround, dlow, pieces)
    near, up, down = sums(sum_y_kernel, ((192, f32), (192, bf16), (128, bf16)), parts_y, token)
    up, down = shift(up, dz=-3), shift(down, dz=3)
    out_y, out_x, token = finish(1, outs, r1, r2, b1, b2, *shared, *local)
    here, left, right = sums(
        sum_z_kernel, ((64, f32), (64, bf16), (64, bf16)), (near, up, down), token
    )
    part = here + shift(right, dz=-1).astype(f32) + shift(left, dz=1).astype(f32)
    part = part.astype(bf16)
    grad_w = sum(
        fetch(part, lambda y, z, c, x, k=k: (y + 2 * ((x + k) % 2), z, c, x + k)).astype(f32)
        for k in range(NX)
    )
    return out_y[None], out_x[None], out_u[None], grad_w


def solution(mesh):
    return jax.shard_map(
        body,
        mesh=mesh,
        in_specs=(
            P("dp", "seq", None), P("dp", "seq", None), P("dp", "seq"), P("dp", "seq", None),
            P("dp", None), P(), P(), P(),
        ),
        out_specs=(P("dp", "seq", None), P("dp", "seq", None), P("dp", "seq", None), P("dp", None)),
        check_vma=False,
    )
```
